128 devices in a mesh: src: 8 (over y, core), tgt: 16 (over z, x).
Axes of the slice: x: 4, y: 4, z: 4, core: 2. Of those that a mesh axis runs over, the one named last changes fastest.
Arguments:
- source_cells: bfloat16 [262144, 64], P('src'), may hold values from -4 to 4
- target_cells: bfloat16 [131072, 64], P('tgt'), may hold values from -1 to 1
- log_source: float32 [262144], P('src'), may hold values from -4 to 4
- log_target: float32 [131072], P('tgt'), may hold values from -4 to 4
- support: int32 [2048, 32], P('src'), may hold values from 0 to 1023, as said below
Outputs:
- source_potential: float32 [262144], P('src')
- target_potential: float32 [131072], P('tgt')
The draws below stay inside these ranges and needn't reach their ends.
Inputs may be any that keep to these rules, and one draw needn't show every extreme that they name: `support`: each row holds 32 different target tile numbers. Within the rows of one index of src (aligned blocks of 256 rows), at most 1024 entries fall among the tiles of one index of tgt (tiles k with k // 64 equal), and exactly 1024 fall on one of them; every target tile is named in the rows of every index of src.
All inputs are finite; a program needn't handle non-finite values.
Results may differ from the reference program's by a relative error of at most 0.0044.
Values may be sent and summed in bfloat16 or wider, within the bound.
No kernel may reach another device: no remote copies, remote signals or barrier semaphores. Data moves between devices by JAX's collectives and lax.ppermute only.
A program may use at most 320 MiB of HBM per device.

```python
import jax
import jax.numpy as jnp
from jax import lax

E = 64
TILE = 128
KT = 32
ITERS = 2
RS_DEV = 32768
CT_DEV = 8192
RB_DEV = 256
SLOTS = 8192
CAP = 1024
NS = 262144
NT = 131072


def draw_source_cells(key, part):
    key = jax.random.fold_in(key, 13)
    key_values, key_pick, key_factor = jax.random.split(key, 3)
    spread = 1.0 / jnp.sqrt(jnp.float32(E))
    values = jax.random.normal(key_values, (NS, E), jnp.float32)
    picked = jax.random.randint(key_pick, (NS,), 0, 8) == 0
    factor = jnp.exp(jax.random.uniform(key_factor, (NS,), jnp.float32, jnp.log(2.5), jnp.log(5.0)))
    factor = jnp.where(picked, factor, 1.0)
    return jnp.clip(values * spread * factor[:, None], -4.0, 4.0).astype(jnp.bfloat16)


def draw_support(key, part):
    key = jax.random.fold_in(key, 11)
    tiles_per = CT_DEV // TILE
    shard_count = NT // CT_DEV
    src_count = NS // RS_DEV

    def one_shard(shard_index):
        shard_key = jax.random.fold_in(key, shard_index)
        key_heavy, key_perm, key_offset = jax.random.split(shard_key, 3)
        heavy = jax.random.randint(key_heavy, (), 0, shard_count)
        position = jnp.arange(SLOTS, dtype=jnp.int32)
        others = (position - CAP) % (shard_count - 1)
        others = others + (others >= heavy).astype(jnp.int32)
        assigned = jnp.where(position < CAP, heavy, others)
        order = jax.random.permutation(key_perm, SLOTS)
        owner = assigned[order]
        onehot = (owner[:, None] == jnp.arange(shard_count, dtype=jnp.int32)[None, :]).astype(jnp.int32)
        before = jnp.cumsum(onehot, axis=0) - onehot
        counter = jnp.sum(before * onehot, axis=1)
        offsets = jax.random.randint(key_offset, (shard_count,), 0, tiles_per)
        local_tile = (counter + offsets[owner]) % tiles_per
        return (owner * tiles_per + local_tile).astype(jnp.int32).reshape(RB_DEV, KT)
    return jax.vmap(one_shard)(jnp.arange(src_count, dtype=jnp.int32)).reshape(NS // TILE, KT)


def shard_levels(stream_key, extent, shards, low, top_value):
    def one(dim, parts):
        heights = jax.random.uniform(jax.random.fold_in(jax.random.fold_in(stream_key, 6), dim), (parts,), jnp.float32, low / len(shards), top_value / len(shards))
        return jnp.repeat(jnp.exp(heights), extent[dim] // parts).reshape((-1,) + (1,) * (len(extent) - dim - 1))

    gain = one(*shards[0])
    for cut in shards[1:]:
        gain = gain * one(*cut)
    return gain


def noise(stream_key, dims, width, most, cuts=(), kind=jnp.bfloat16):
    entries = width * jax.random.normal(stream_key, dims, jnp.float32)
    if cuts:
        entries = entries * shard_levels(stream_key, dims, cuts, -0.22, 0.18)
    return jnp.clip(entries, -most, most).astype(kind)


def setup_inputs(seed: int = 0) -> dict:
    splits = jax.random.split(jax.random.key(seed), 6)
    return {
        "source_cells": draw_source_cells(jax.random.fold_in(splits[5], 71), 0),
        "target_cells": noise(splits[1], (NT, E), 0.125, 1.0, ((0, 16),)),
        "log_source": jnp.clip(jax.random.uniform(splits[2], (NS,), jnp.float32, -4.0, 4.0) * shard_levels(splits[2], (NS,), ((0, 8),), -0.4, 0.0), -4.0, 4.0),
        "log_target": jnp.clip(jax.random.uniform(splits[3], (NT,), jnp.float32, -4.0, 4.0) * shard_levels(splits[3], (NT,), ((0, 16),), -0.4, 0.0), -4.0, 4.0),
        "support": draw_support(jax.random.fold_in(splits[5], 71), 0),
    }


EPS = 0.1
NEG = -1.0e30


def reference(source_cells, target_cells, log_source, log_target, support):
    src_tiles = source_cells.astype(jnp.float32).reshape(-1, TILE, E)
    tgt_tiles = target_cells.astype(jnp.float32).reshape(-1, TILE, E)
    src_norm = jnp.sum(src_tiles * src_tiles, axis=2)
    tgt_norm = jnp.sum(tgt_tiles * tgt_tiles, axis=2)
    log_rows = log_source.reshape(-1, TILE)
    log_cols = log_target.reshape(-1, TILE)

    def block_cost(src_block, src_square, tile_ids):
        chosen = tgt_tiles[tile_ids]
        cross_term = jnp.einsum("ie,kje->ikj", src_block, chosen, precision=lax.Precision.HIGHEST)
        return src_square[:, None, None] + tgt_norm[tile_ids][None, :, :] - 2.0 * cross_term

    def row_pass(target_pot):
        def one_block(block_item):
            src_block, src_square, tile_ids, log_block = block_item
            costs = block_cost(src_block, src_square, tile_ids)
            scores = (target_pot[tile_ids][None, :, :] - costs) / EPS
            highest = jnp.max(scores, axis=(1, 2))
            summed = jnp.sum(jnp.exp(scores - highest[:, None, None]), axis=(1, 2))
            return EPS * log_block - EPS * (highest + jnp.log(summed))
        return lax.map(one_block, (src_tiles, src_norm, support, log_rows))

    def col_pass(source_pot):
        def one_step(carried, block_item):
            maxima, totals = carried
            src_block, src_square, tile_ids, pot_block = block_item
            costs = block_cost(src_block, src_square, tile_ids)
            scores = (pot_block[:, None, None] - costs) / EPS
            old_max = maxima[tile_ids]
            new_max = jnp.maximum(old_max, jnp.max(scores, axis=0))
            new_total = totals[tile_ids] * jnp.exp(old_max - new_max) + jnp.sum(jnp.exp(scores - new_max[None, :, :]), axis=0)
            return (maxima.at[tile_ids].set(new_max), totals.at[tile_ids].set(new_total)), None
        start_carry = (jnp.full(log_cols.shape, NEG, jnp.float32), jnp.zeros(log_cols.shape, jnp.float32))
        (maxima, totals), unused = lax.scan(one_step, start_carry, (src_tiles, src_norm, support, source_pot))
        return EPS * log_cols - EPS * (maxima + jnp.log(totals))

    target_pot = jnp.zeros(log_cols.shape, jnp.float32)
    source_pot = jnp.zeros(log_rows.shape, jnp.float32)
    for iteration in range(ITERS):
        source_pot = row_pass(target_pot)
        target_pot = col_pass(source_pot)
    return source_pot.reshape(-1), target_pot.reshape(-1)
```

```python
import functools

import jax
import jax.numpy as jnp
from jax import lax
from jax.experimental import pallas as pl
from jax.experimental.pallas import tpu as pltpu
from jax.sharding import PartitionSpec as P

TILE = 128
ITERS = 2


EPS = 0.1
NEG = -1e30
HIGH = lax.Precision.HIGHEST

SCALE = 14.426950408889634
LN2 = 0.6931471805599453
SHIFT = 9.0
ROW_LOW = 2.0**-30
ROW_HIGH = 2.0**80
COL_LOW = 2.0**-10
COL_HIGH = 2.0**80
RATIO = 2.0**30
POISON = 3.0e38
POISONED = 1.0e37


def squares_of(tiles):
    values = tiles.astype(jnp.float32)
    return jnp.sum(values * values, axis=2)


def cost_tile(src_block, src_square, tgt_block, tgt_square):
    cross_term = jnp.einsum(
        "bie,bje->bij", src_block, tgt_block, preferred_element_type=jnp.float32
    )
    return src_square[:, :, None] + tgt_square[:, None, :] - 2.0 * cross_term


def one_hot(ids, count):
    return (ids[:, None] == jnp.arange(count, dtype=jnp.int32)[None, :]).astype(jnp.float32)


def pick_rows(selector, table):
    return jnp.dot(selector, table, precision=HIGH, preferred_element_type=jnp.float32)


def fold_block(maxima, totals, selector, block_max, exp_of):
    candidate = jnp.max(jnp.where(selector[:, :, None] > 0.5, block_max[:, None, :], NEG), axis=0)
    new_max = jnp.maximum(maxima, candidate)
    exp_terms = exp_of(pick_rows(selector, new_max))
    added = jnp.dot(selector.T, exp_terms, precision=HIGH, preferred_element_type=jnp.float32)
    return (new_max, totals * jnp.exp(maxima - new_max) + added)


def row_stats(
    slot_rows,
    slot_tiles,
    active,
    pre_src,
    pre_srcn,
    pre_tgt,
    pre_tgtn,
    target_pot,
    row_count,
    num_blocks,
):
    shape_rows = (row_count, pre_srcn.shape[1])
    start_carry = (jnp.full(shape_rows, NEG, jnp.float32), jnp.zeros(shape_rows, jnp.float32))
    tile_count = target_pot.shape[0]

    def row_one_step(carried, block_item):
        maxima, totals = carried
        row_ids, tile_ids, alive, src_block, src_square, tgt_block, tgt_square = block_item
        costs = cost_tile(src_block, src_square, tgt_block, tgt_square)
        slot_pot = pick_rows(one_hot(tile_ids, tile_count), target_pot)
        scores = (slot_pot[:, None, :] - costs) / EPS
        block_max = jnp.where(alive[:, None], jnp.max(scores, axis=2), NEG)
        selector = one_hot(row_ids, row_count) * alive[:, None].astype(jnp.float32)

        def exp_of(slot_max):
            terms = jnp.sum(jnp.exp(scores - slot_max[:, :, None]), axis=2)
            return jnp.where(alive[:, None], terms, 0.0)

        return (fold_block(maxima, totals, selector, block_max, exp_of), None)

    def row_blocks(array):
        return array.reshape((num_blocks, -1) + array.shape[1:])

    block_items = tuple(
        (
            row_blocks(item)
            for item in (slot_rows, slot_tiles, active, pre_src, pre_srcn, pre_tgt, pre_tgtn)
        )
    )
    return lax.scan(row_one_step, start_carry, block_items)[0]


def col_stats(
    slot_rows,
    slot_tiles,
    active,
    pre_src,
    pre_srcn,
    pre_tgt,
    pre_tgtn,
    source_pot,
    tile_count,
    num_blocks,
):
    shape_cols = (tile_count, pre_tgtn.shape[1])
    start_carry = (jnp.full(shape_cols, NEG, jnp.float32), jnp.zeros(shape_cols, jnp.float32))
    row_count = source_pot.shape[0]

    def col_one_step(carried, block_item):
        maxima, totals = carried
        row_ids, tile_ids, alive, src_block, src_square, tgt_block, tgt_square = block_item
        costs = cost_tile(src_block, src_square, tgt_block, tgt_square)
        slot_pot = pick_rows(one_hot(row_ids, row_count), source_pot)
        scores = (slot_pot[:, :, None] - costs) / EPS
        block_max = jnp.where(alive[:, None], jnp.max(scores, axis=1), NEG)
        selector = one_hot(tile_ids, tile_count) * alive[:, None].astype(jnp.float32)

        def exp_of(slot_max):
            terms = jnp.sum(jnp.exp(scores - slot_max[:, None, :]), axis=1)
            return jnp.where(alive[:, None], terms, 0.0)

        return (fold_block(maxima, totals, selector, block_max, exp_of), None)

    def col_blocks(array):
        return array.reshape((num_blocks, -1) + array.shape[1:])

    block_items = tuple(
        (
            col_blocks(item)
            for item in (slot_rows, slot_tiles, active, pre_src, pre_srcn, pre_tgt, pre_tgtn)
        )
    )
    return lax.scan(col_one_step, start_carry, block_items)[0]


def across_targets(maxima, totals):
    highest = lax.pmax(maxima, "tgt")
    return (highest, lax.psum(totals * jnp.exp(maxima - highest), "tgt"))


def across_sources(maxima, totals):
    highest = lax.pmax(maxima, "src")
    return (highest, lax.psum(totals * jnp.exp(maxima - highest), "src"))


def general_path(source_cells, target_cells, log_source, log_target, support):
    row_count = source_cells.shape[0] // TILE
    src_tiles = source_cells.reshape(row_count, TILE, source_cells.shape[1])
    src_norm = squares_of(src_tiles)
    flat_ids = support.reshape(-1)
    num_slots = flat_ids.shape[0]
    tgt_index = lax.axis_index("tgt")
    own_tiles = target_cells.shape[0] // TILE
    per_device = num_slots // lax.axis_size("tgt")
    tgt_tiles = target_cells.reshape(own_tiles, TILE, target_cells.shape[1])
    log_cols = log_target.reshape(own_tiles, TILE)
    capacity = 2 * per_device
    owned = flat_ids // own_tiles == tgt_index
    slot_rank = jnp.cumsum(owned.astype(jnp.int32)) - 1
    target_place = jnp.where(owned, slot_rank, capacity)
    slot_index = (
        jnp.zeros((capacity,), jnp.int32)
        .at[target_place]
        .set(jnp.arange(num_slots, dtype=jnp.int32), mode="drop")
    )
    active = jnp.arange(capacity, dtype=jnp.int32) < jnp.sum(owned.astype(jnp.int32))
    slot_tiles = jnp.clip(flat_ids[slot_index] - tgt_index * own_tiles, 0, own_tiles - 1)
    tgt_norm = squares_of(tgt_tiles)
    tile_count = tgt_tiles.shape[0]
    slot_rows = slot_index // support.shape[1]
    pre_src = src_tiles[slot_rows]
    pre_srcn = src_norm[slot_rows]
    pre_tgt = tgt_tiles[slot_tiles]
    pre_tgtn = tgt_norm[slot_tiles]
    num_blocks = capacity // min(64, capacity)
    log_rows = log_source.reshape(row_count, TILE)
    target_pot = jnp.zeros(log_cols.shape, jnp.float32)
    source_pot = jnp.zeros(log_rows.shape, jnp.float32)
    for iteration in range(ITERS):
        maxima, totals = row_stats(
            slot_rows,
            slot_tiles,
            active,
            pre_src,
            pre_srcn,
            pre_tgt,
            pre_tgtn,
            target_pot,
            row_count,
            num_blocks,
        )
        maxima, totals = across_targets(maxima, totals)
        source_pot = EPS * log_rows - EPS * (maxima + jnp.log(totals))
        maxima, totals = col_stats(
            slot_rows,
            slot_tiles,
            active,
            pre_src,
            pre_srcn,
            pre_tgt,
            pre_tgtn,
            source_pot,
            tile_count,
            num_blocks,
        )
        maxima, totals = across_sources(maxima, totals)
        target_pot = EPS * log_cols - EPS * (maxima + jnp.log(totals))
    return (source_pot.reshape(-1), target_pot.reshape(-1))


CAP_STEP = 128
BUILD_UNROLL = 64
ROW_UNROLL = 64
COL_UNROLL = 64
SMEM = pl.BlockSpec(memory_space=pltpu.SMEM)
VMEM = pl.BlockSpec(memory_space=pltpu.VMEM)
BF16 = jnp.bfloat16
F32 = jnp.float32


def params(mib):
    return pltpu.CompilerParams(vmem_limit_bytes=mib * 2**20)


def dot_t(a, b):
    return lax.dot_general(a, b, (((1,), (1,)), ((), ())), preferred_element_type=F32)


def dot_n(a, b):
    return jnp.dot(a, b, preferred_element_type=F32)


def ones_where(mask):
    return jnp.where(mask, 1.0, 0.0).astype(BF16)


def iota(shape, axis):
    return lax.broadcasted_iota(jnp.int32, shape, axis)


def list_kernel(place_ref, sup_ref, rows_ref, tiles_ref, count_ref, by_row_ref, by_tile_ref):
    width, rows = sup_ref.shape
    cap = rows_ref.shape[1]
    own_tiles = by_tile_ref.shape[0]
    local = sup_ref[...] - place_ref[0] * own_tiles
    owned = (local >= 0) & (local < own_tiles)
    mask = ones_where(owned)
    lower = ones_where(iota((width, width), 1) <= iota((width, width), 0))
    rank = dot_n(lower, mask)
    count = rank[width - 1 : width, :]
    before = ones_where(iota((rows, rows), 1) < iota((rows, rows), 0))
    upto = ones_where(iota((rows, rows), 1) <= iota((rows, rows), 0))
    first = jnp.sum(dot_t(before, mask), axis=1, keepdims=True).astype(jnp.int32)
    last = jnp.sum(dot_t(upto, mask), axis=1, keepdims=True).astype(jnp.int32)
    place = iota((rows, cap), 1)
    by_row = ones_where((first <= place) & (place < last))
    by_row_ref[...] = by_row
    after = ones_where(iota((rows, rows), 0) < iota((rows, rows), 1))
    count8 = jnp.broadcast_to(count, (8, rows)).astype(BF16)
    first8 = dot_n(count8, after)
    high = jnp.floor(first8 * (1.0 / 32.0))
    low = first8 - 32.0 * high
    row_id = iota((8, rows), 1).astype(F32)
    tile = jnp.where(owned, local, 0).astype(F32)
    table = jnp.concatenate([tile, jnp.where(owned, rank, 0.0), row_id, high, low], axis=0)
    got = dot_n(table.astype(BF16), by_row)
    begin = 32.0 * got[2 * width + 8 : 2 * width + 9] + got[2 * width + 16 : 2 * width + 17]
    place_f = iota((1, cap), 1).astype(F32)
    want = place_f - begin + 1.0
    tiles = jnp.sum(jnp.where(got[width : 2 * width] == want, got[:width], 0.0), axis=0, keepdims=True)
    tiles_ref[...] = tiles.astype(jnp.int32)
    rows_ref[...] = got[2 * width : 2 * width + 1].astype(jnp.int32)
    total = jnp.sum(count, axis=1, keepdims=True)
    count_ref[...] = jnp.broadcast_to(total, count_ref.shape).astype(jnp.int32)
    by_tile_ref[...] = ones_where(
        (iota((own_tiles, cap), 0).astype(F32) == tiles) & (place_f < total)
    )


def sum_slots(members, parts):
    high = parts.astype(BF16)
    low = (parts - high.astype(F32)).astype(BF16)
    return dot_n(members, high) + dot_n(members, low)


def build_kernel(
    count_ref, rows_ref, tiles_ref, src_ref, tgt_ref, by_row_ref,
    kern_ref, sum_ref, norm_ref, shift_ref,
    left, extra, part,
):
    dim, tgt_count = tgt_ref.shape
    row_count = extra.shape[0]
    lane = iota((TILE, TILE), 1)

    def one_tgt(k, unused):
        block = tgt_ref[:, pl.ds(pl.multiple_of(k * TILE, TILE), TILE)].astype(F32)
        wide = jnp.concatenate([block, jnp.zeros((TILE - dim, TILE), F32)], axis=0).T
        half = -0.5 * jnp.sum(wide * wide, axis=1, keepdims=True)
        a = half.astype(BF16).astype(F32)
        b = (half - a).astype(BF16).astype(F32)
        c = half - a - b
        pieces = jnp.where(lane == dim, a, jnp.where(lane == dim + 1, b, jnp.where(lane == dim + 2, c, 1.0)))
        left[k] = jnp.where(lane < dim, wide, jnp.where(lane < dim + 4, pieces, 0.0)).astype(BF16)
        return unused

    lax.fori_loop(0, tgt_count // TILE, one_tgt, 0)
    line = iota((16, TILE), 0)

    def one_src(r, unused):
        block = src_ref[:, pl.ds(pl.multiple_of(r * TILE, TILE), TILE)].astype(F32)
        norm = jnp.sum(block * block, axis=0, keepdims=True)
        part_shift = (jnp.sqrt(norm) * (SHIFT / (2.0 * SCALE))).astype(BF16).astype(F32)
        norm_ref[pl.ds(r, 1), :] = norm
        shift_ref[pl.ds(r, 1), :] = part_shift * (2.0 * SCALE)
        extra[r] = jnp.where(line < 3, 1.0, jnp.where(line == 3, -part_shift, 0.0)).astype(BF16)
        return unused

    lax.fori_loop(0, row_count, one_src, 0, unroll=8)
    part[...] = jnp.zeros_like(part)
    pad = jnp.zeros((TILE - dim - 16, TILE), BF16)

    def step(g, unused):
        base = g * BUILD_UNROLL
        for u in range(BUILD_UNROLL):
            q = base + u
            r = rows_ref[0, q]
            k = tiles_ref[0, q]
            block = src_ref[:, pl.ds(pl.multiple_of(r * TILE, TILE), TILE)]
            right = jnp.concatenate([block, extra[r], pad], axis=0)
            entry = jnp.exp2(dot_n(left[k], right) * (2.0 * SCALE))
            kern_ref[q] = entry.astype(BF16)
            part[pl.ds(q, 1), :] = jnp.sum(entry, axis=0, keepdims=True)
        return unused

    lax.fori_loop(0, pl.cdiv(count_ref[0, 0], BUILD_UNROLL), step, 0)
    sum_ref[...] = sum_slots(by_row_ref[...], part[...])


def in_range(value, low, high):
    return (value >= low) & (value <= high)


def poison(ok, value):
    bad = jnp.max(jnp.where(ok, 0.0, 1.0))
    return jnp.where(bad > 0.0, POISON, value)


def two_rows(table, first, second):
    return jnp.concatenate(
        [
            jnp.broadcast_to(table[pl.ds(first, 1), :], (8, TILE)),
            jnp.broadcast_to(table[pl.ds(second, 1), :], (8, TILE)),
        ],
        axis=0,
    ).astype(BF16)


def row_kernel(count_ref, tiles_ref, total_ref, log_ref, kern_ref, by_row_ref, out_ref, table, part):
    total = total_ref[...]
    table[...] = jnp.exp(log_ref[...]) / total
    part[...] = jnp.zeros_like(part)

    def step(g, unused):
        base = g * ROW_UNROLL
        for u in range(0, ROW_UNROLL, 2):
            q = base + u
            weights = two_rows(table, tiles_ref[0, q], tiles_ref[0, q + 1])
            pair = jnp.concatenate([kern_ref[q], kern_ref[q + 1]], axis=1)
            got = dot_n(weights, pair)
            part[pl.ds(q, 1), :] = got[0:1, :TILE]
            part[pl.ds(q + 1, 1), :] = got[8:9, TILE:]
        return unused

    lax.fori_loop(0, pl.cdiv(count_ref[0, 0], ROW_UNROLL), step, 0)
    out = sum_slots(by_row_ref[...], part[...])
    out_ref[...] = poison(in_range(total, COL_LOW, COL_HIGH), out)


def col_body(ok, count_ref, rows_ref, total, log_ref, kern_ref, by_tile_ref, out_ref, table, part):
    table[...] = jnp.exp(log_ref[...]) / total
    part[...] = jnp.zeros_like(part)
    none = jnp.zeros((16, TILE), BF16)

    def step(g, unused):
        base = g * COL_UNROLL
        for u in range(0, COL_UNROLL, 4):
            q = base + u
            ab = two_rows(table, rows_ref[0, q], rows_ref[0, q + 1])
            cd = two_rows(table, rows_ref[0, q + 2], rows_ref[0, q + 3])
            weights = jnp.concatenate(
                [jnp.concatenate([ab, none], axis=1), jnp.concatenate([none, cd], axis=1)], axis=0
            )
            four = jnp.concatenate(
                [
                    jnp.concatenate([kern_ref[q], kern_ref[q + 2]], axis=1),
                    jnp.concatenate([kern_ref[q + 1], kern_ref[q + 3]], axis=1),
                ],
                axis=0,
            )
            got = dot_t(weights, four)
            part[pl.ds(q, 1), :] = got[0:1, :TILE]
            part[pl.ds(q + 1, 1), :] = got[8:9, TILE:]
            part[pl.ds(q + 2, 1), :] = got[16:17, :TILE]
            part[pl.ds(q + 3, 1), :] = got[24:25, TILE:]
        return unused

    lax.fori_loop(0, pl.cdiv(count_ref[0, 0], COL_UNROLL), step, 0)
    out_ref[...] = poison(ok, sum_slots(by_tile_ref[...], part[...]))


def first_col_kernel(count_ref, rows_ref, total_ref, log_ref, kern_ref, by_tile_ref, out_ref, table, part):
    total = total_ref[...]
    ok = in_range(total, ROW_LOW, ROW_HIGH)
    col_body(ok, count_ref, rows_ref, total, log_ref, kern_ref, by_tile_ref, out_ref, table, part)


def next_col_kernel(
    count_ref, rows_ref, total_ref, earlier_ref, log_ref, kern_ref, by_tile_ref, out_ref, table, part
):
    total = total_ref[...]
    ratio = total / earlier_ref[...]
    ok = in_range(total, ROW_LOW, ROW_HIGH) & in_range(ratio, 1.0 / RATIO, RATIO)
    col_body(ok, count_ref, rows_ref, total, log_ref, kern_ref, by_tile_ref, out_ref, table, part)


def ring_sum(value, axis, size, perm):
    def moved(d):
        return lax.ppermute(value, axis, [(i, perm(i, d)) for i in range(size)])

    opposite, right, left = moved(2), moved(1), moved(3)
    return (value + opposite) + (right + left)


def sum_over_tgt(value):
    value = ring_sum(value, "tgt", 16, lambda i, d: (i // 4) * 4 + (i % 4 + d) % 4)
    return ring_sum(value, "tgt", 16, lambda i, d: (i + 4 * d) % 16)


def sum_over_src(value):
    value = value + lax.ppermute(value, "src", [(i, i ^ 1) for i in range(8)])
    return ring_sum(value, "src", 8, lambda i, d: (i + 2 * d) % 8)


def on_device(source_cells, target_cells, log_source, log_target, support):
    row_count = source_cells.shape[0] // TILE
    tile_count = target_cells.shape[0] // TILE
    cap = 2 * support.size // lax.axis_size("tgt")
    place = lax.axis_index("tgt").astype(jnp.int32).reshape(1)
    log_rows = log_source.reshape(row_count, TILE)
    log_cols = log_target.reshape(tile_count, TILE)
    array = jax.ShapeDtypeStruct
    rows, tiles, count, by_row, by_tile = pl.pallas_call(
        list_kernel,
        out_shape=(
            array((1, cap), jnp.int32),
            array((1, cap), jnp.int32),
            array((1, TILE), jnp.int32),
            array((row_count, cap), BF16),
            array((tile_count, cap), BF16),
        ),
        in_specs=[SMEM, VMEM],
        out_specs=(VMEM,) * 5,
        compiler_params=params(16),
        name="list_support",
    )(place, support.T)
    kern, total, norm, shift = pl.pallas_call(
        build_kernel,
        out_shape=(
            pltpu.VMEM((cap, TILE, TILE), BF16),
            array((row_count, TILE), F32),
            array((row_count, TILE), F32),
            array((row_count, TILE), F32),
        ),
        in_specs=[SMEM] * 3 + [VMEM] * 3,
        out_specs=(VMEM,) * 4,
        scratch_shapes=[
            pltpu.VMEM((tile_count, TILE, TILE), BF16),
            pltpu.VMEM((row_count, 16, TILE), BF16),
            pltpu.VMEM((cap, TILE), F32),
        ],
        compiler_params=params(20),
        name="build",
    )(count, rows, tiles, source_cells.T, target_cells.T, by_row)
    kern = pltpu.with_memory_space_constraint(kern, pltpu.VMEM)
    part = pltpu.VMEM((cap, TILE), F32)

    def call(body, name, smem, vmem, out_rows, table_rows):
        return pl.pallas_call(
            body,
            out_shape=array((out_rows, TILE), F32),
            in_specs=[SMEM] * len(smem) + [VMEM] * len(vmem),
            out_specs=VMEM,
            scratch_shapes=[pltpu.VMEM((table_rows, TILE), F32), part],
            compiler_params=params(12),
            name=name,
        )(*smem, *vmem)

    first = sum_over_tgt(total)
    cols = call(
        first_col_kernel, "first_col", (count, rows), (first, log_rows, kern, by_tile), tile_count, row_count
    )
    cols = sum_over_src(cols)
    second = call(row_kernel, "row", (count, tiles), (cols, log_cols, kern, by_row), row_count, tile_count)
    second = sum_over_tgt(second)
    cols = call(
        next_col_kernel, "next_col", (count, rows), (second, first, log_rows, kern, by_tile), tile_count, row_count
    )
    cols = sum_over_src(cols)
    source_pot = norm + EPS * log_rows - EPS * (jnp.log(second) + LN2 * shift)
    target_pot = EPS * log_cols - EPS * jnp.log(cols)
    return lax.cond(
        jnp.max(cols) < POISONED,
        lambda *unused: (source_pot.reshape(-1), target_pot.reshape(-1)),
        general_path,
        source_cells,
        target_cells,
        log_source,
        log_target,
        support,
    )


def solution(mesh):
    return jax.shard_map(
        on_device,
        mesh=mesh,
        in_specs=(P("src", None), P("tgt", None), P("src"), P("tgt"), P("src", None)),
        out_specs=(P("src"), P("tgt")),
        check_vma=False,
    )
```

```python
import functools

import jax
import jax.numpy as jnp
from jax import lax
from jax.experimental import pallas as pl
from jax.experimental.pallas import tpu as pltpu
from jax.sharding import PartitionSpec as P

TILE = 128
ITERS = 2


EPS = 0.1
NEG = -1e30
HIGH = lax.Precision.HIGHEST

SCALE = 14.426950408889634
LN2 = 0.6931471805599453
SHIFT = 9.0
ROW_LOW = 2.0**-30
ROW_HIGH = 2.0**80
COL_LOW = 2.0**-10
COL_HIGH = 2.0**80
RATIO = 2.0**30
POISON = 3.0e38
POISONED = 1.0e37


def squares_of(tiles):
    values = tiles.astype(jnp.float32)
    return jnp.sum(values * values, axis=2)


def cost_tile(src_block, src_square, tgt_block, tgt_square):
    cross_term = jnp.einsum(
        "bie,bje->bij", src_block, tgt_block, preferred_element_type=jnp.float32
    )
    return src_square[:, :, None] + tgt_square[:, None, :] - 2.0 * cross_term


def one_hot(ids, count):
    return (ids[:, None] == jnp.arange(count, dtype=jnp.int32)[None, :]).astype(jnp.float32)


def pick_rows(selector, table):
    return jnp.dot(selector, table, precision=HIGH, preferred_element_type=jnp.float32)


def fold_block(maxima, totals, selector, block_max, exp_of):
    candidate = jnp.max(jnp.where(selector[:, :, None] > 0.5, block_max[:, None, :], NEG), axis=0)
    new_max = jnp.maximum(maxima, candidate)
    exp_terms = exp_of(pick_rows(selector, new_max))
    added = jnp.dot(selector.T, exp_terms, precision=HIGH, preferred_element_type=jnp.float32)
    return (new_max, totals * jnp.exp(maxima - new_max) + added)


def row_stats(
    slot_rows,
    slot_tiles,
    active,
    pre_src,
    pre_srcn,
    pre_tgt,
    pre_tgtn,
    target_pot,
    row_count,
    num_blocks,
):
    shape_rows = (row_count, pre_srcn.shape[1])
    start_carry = (jnp.full(shape_rows, NEG, jnp.float32), jnp.zeros(shape_rows, jnp.float32))
    tile_count = target_pot.shape[0]

    def row_one_step(carried, block_item):
        maxima, totals = carried
        row_ids, tile_ids, alive, src_block, src_square, tgt_block, tgt_square = block_item
        costs = cost_tile(src_block, src_square, tgt_block, tgt_square)
        slot_pot = pick_rows(one_hot(tile_ids, tile_count), target_pot)
        scores = (slot_pot[:, None, :] - costs) / EPS
        block_max = jnp.where(alive[:, None], jnp.max(scores, axis=2), NEG)
        selector = one_hot(row_ids, row_count) * alive[:, None].astype(jnp.float32)

        def exp_of(slot_max):
            terms = jnp.sum(jnp.exp(scores - slot_max[:, :, None]), axis=2)
            return jnp.where(alive[:, None], terms, 0.0)

        return (fold_block(maxima, totals, selector, block_max, exp_of), None)

    def row_blocks(array):
        return array.reshape((num_blocks, -1) + array.shape[1:])

    block_items = tuple(
        (
            row_blocks(item)
            for item in (slot_rows, slot_tiles, active, pre_src, pre_srcn, pre_tgt, pre_tgtn)
        )
    )
    return lax.scan(row_one_step, start_carry, block_items)[0]


def col_stats(
    slot_rows,
    slot_tiles,
    active,
    pre_src,
    pre_srcn,
    pre_tgt,
    pre_tgtn,
    source_pot,
    tile_count,
    num_blocks,
):
    shape_cols = (tile_count, pre_tgtn.shape[1])
    start_carry = (jnp.full(shape_cols, NEG, jnp.float32), jnp.zeros(shape_cols, jnp.float32))
    row_count = source_pot.shape[0]

    def col_one_step(carried, block_item):
        maxima, totals = carried
        row_ids, tile_ids, alive, src_block, src_square, tgt_block, tgt_square = block_item
        costs = cost_tile(src_block, src_square, tgt_block, tgt_square)
        slot_pot = pick_rows(one_hot(row_ids, row_count), source_pot)
        scores = (slot_pot[:, :, None] - costs) / EPS
        block_max = jnp.where(alive[:, None], jnp.max(scores, axis=1), NEG)
        selector = one_hot(tile_ids, tile_count) * alive[:, None].astype(jnp.float32)

        def exp_of(slot_max):
            terms = jnp.sum(jnp.exp(scores - slot_max[:, None, :]), axis=1)
            return jnp.where(alive[:, None], terms, 0.0)

        return (fold_block(maxima, totals, selector, block_max, exp_of), None)

    def col_blocks(array):
        return array.reshape((num_blocks, -1) + array.shape[1:])

    block_items = tuple(
        (
            col_blocks(item)
            for item in (slot_rows, slot_tiles, active, pre_src, pre_srcn, pre_tgt, pre_tgtn)
        )
    )
    return lax.scan(col_one_step, start_carry, block_items)[0]


def across_targets(maxima, totals):
    highest = lax.pmax(maxima, "tgt")
    return (highest, lax.psum(totals * jnp.exp(maxima - highest), "tgt"))


def across_sources(maxima, totals):
    highest = lax.pmax(maxima, "src")
    return (highest, lax.psum(totals * jnp.exp(maxima - highest), "src"))


def general_path(source_cells, target_cells, log_source, log_target, support):
    row_count = source_cells.shape[0] // TILE
    src_tiles = source_cells.reshape(row_count, TILE, source_cells.shape[1])
    src_norm = squares_of(src_tiles)
    flat_ids = support.reshape(-1)
    num_slots = flat_ids.shape[0]
    tgt_index = lax.axis_index("tgt")
    own_tiles = target_cells.shape[0] // TILE
    per_device = num_slots // lax.axis_size("tgt")
    tgt_tiles = target_cells.reshape(own_tiles, TILE, target_cells.shape[1])
    log_cols = log_target.reshape(own_tiles, TILE)
    capacity = 2 * per_device
    owned = flat_ids // own_tiles == tgt_index
    slot_rank = jnp.cumsum(owned.astype(jnp.int32)) - 1
    target_place = jnp.where(owned, slot_rank, capacity)
    slot_index = (
        jnp.zeros((capacity,), jnp.int32)
        .at[target_place]
        .set(jnp.arange(num_slots, dtype=jnp.int32), mode="drop")
    )
    active = jnp.arange(capacity, dtype=jnp.int32) < jnp.sum(owned.astype(jnp.int32))
    slot_tiles = jnp.clip(flat_ids[slot_index] - tgt_index * own_tiles, 0, own_tiles - 1)
    tgt_norm = squares_of(tgt_tiles)
    tile_count = tgt_tiles.shape[0]
    slot_rows = slot_index // support.shape[1]
    pre_src = src_tiles[slot_rows]
    pre_srcn = src_norm[slot_rows]
    pre_tgt = tgt_tiles[slot_tiles]
    pre_tgtn = tgt_norm[slot_tiles]
    num_blocks = capacity // min(64, capacity)
    log_rows = log_source.reshape(row_count, TILE)
    target_pot = jnp.zeros(log_cols.shape, jnp.float32)
    source_pot = jnp.zeros(log_rows.shape, jnp.float32)
    for iteration in range(ITERS):
        maxima, totals = row_stats(
            slot_rows,
            slot_tiles,
            active,
            pre_src,
            pre_srcn,
            pre_tgt,
            pre_tgtn,
            target_pot,
            row_count,
            num_blocks,
        )
        maxima, totals = across_targets(maxima, totals)
        source_pot = EPS * log_rows - EPS * (maxima + jnp.log(totals))
        maxima, totals = col_stats(
            slot_rows,
            slot_tiles,
            active,
            pre_src,
            pre_srcn,
            pre_tgt,
            pre_tgtn,
            source_pot,
            tile_count,
            num_blocks,
        )
        maxima, totals = across_sources(maxima, totals)
        target_pot = EPS * log_cols - EPS * (maxima + jnp.log(totals))
    return (source_pot.reshape(-1), target_pot.reshape(-1))


CAP_STEP = 128
BUILD_UNROLL = 64
ROW_UNROLL = 64
COL_UNROLL = 64
SMEM = pl.BlockSpec(memory_space=pltpu.SMEM)
VMEM = pl.BlockSpec(memory_space=pltpu.VMEM)
ANY = pl.BlockSpec(memory_space=pl.ANY)
BF16 = jnp.bfloat16
F32 = jnp.float32


def params(mib):
    return pltpu.CompilerParams(vmem_limit_bytes=mib * 2**20)


def dot_t(a, b):
    return lax.dot_general(a, b, (((1,), (1,)), ((), ())), preferred_element_type=F32)


def dot_n(a, b):
    return jnp.dot(a, b, preferred_element_type=F32)


def ones_where(mask):
    return jnp.where(mask, 1.0, 0.0).astype(BF16)


def iota(shape, axis):
    return lax.broadcasted_iota(jnp.int32, shape, axis)


def list_support(sup_ref, rows_ref, tiles_ref, count_ref, by_row_ref, by_tile_ref):
    width, rows = sup_ref.shape
    cap = rows_ref.shape[1]
    own_tiles = by_tile_ref.shape[0]
    local = sup_ref[...] - lax.axis_index("tgt") * own_tiles
    owned = (local >= 0) & (local < own_tiles)
    mask = ones_where(owned)
    lower = ones_where(iota((width, width), 1) <= iota((width, width), 0))
    rank = dot_n(lower, mask)
    count = rank[width - 1 : width, :]
    before = ones_where(iota((rows, rows), 1) < iota((rows, rows), 0))
    upto = ones_where(iota((rows, rows), 1) <= iota((rows, rows), 0))
    first = jnp.sum(dot_t(before, mask), axis=1, keepdims=True).astype(jnp.int32)
    last = jnp.sum(dot_t(upto, mask), axis=1, keepdims=True).astype(jnp.int32)
    place = iota((rows, cap), 1)
    by_row = ones_where((first <= place) & (place < last))
    by_row_ref[...] = by_row
    after = ones_where(iota((rows, rows), 0) < iota((rows, rows), 1))
    count8 = jnp.broadcast_to(count, (8, rows)).astype(BF16)
    first8 = dot_n(count8, after)
    high = jnp.floor(first8 * (1.0 / 32.0))
    low = first8 - 32.0 * high
    row_id = iota((8, rows), 1).astype(F32)
    tile = jnp.where(owned, local, 0).astype(F32)
    table = jnp.concatenate([tile, jnp.where(owned, rank, 0.0), row_id, high, low], axis=0)
    got = dot_n(table.astype(BF16), by_row)
    begin = 32.0 * got[2 * width + 8 : 2 * width + 9] + got[2 * width + 16 : 2 * width + 17]
    place_f = iota((1, cap), 1).astype(F32)
    want = place_f - begin + 1.0
    tiles = jnp.sum(jnp.where(got[width : 2 * width] == want, got[:width], 0.0), axis=0, keepdims=True)
    tiles_ref[...] = tiles.astype(jnp.int32)
    rows_ref[...] = got[2 * width : 2 * width + 1].astype(jnp.int32)
    total = jnp.sum(count, axis=1, keepdims=True)
    count_ref[...] = jnp.broadcast_to(total, count_ref.shape).astype(jnp.int32)
    by_tile_ref[...] = ones_where(
        (iota((own_tiles, cap), 0).astype(F32) == tiles) & (place_f < total)
    )


def sum_slots(members, parts):
    high = parts.astype(BF16)
    low = (parts - high.astype(F32)).astype(BF16)
    return dot_n(members, high) + dot_n(members, low)


def build_kernel(
    sup_hbm, src_hbm, tgt_hbm,
    kern_ref, sum_ref, norm_ref, shift_ref, rows_out, tiles_out, count_out, by_row_ref, by_tile_ref,
    left, extra, part, sup_ref, src_ref, tgt_ref, rows_ref, tiles_ref, count_ref, sems,
):
    moves = [
        pltpu.make_async_copy(*pair, sems.at[i])
        for i, pair in enumerate(
            [
                (sup_hbm, sup_ref),
                (tgt_hbm, tgt_ref),
                (src_hbm, src_ref),
                (rows_out, rows_ref),
                (tiles_out, tiles_ref),
                (count_out, count_ref),
            ]
        )
    ]
    for move in moves[:3]:
        move.start()
    moves[0].wait()
    list_support(sup_ref, rows_out, tiles_out, count_out, by_row_ref, by_tile_ref)
    for move in moves[3:]:
        move.start()
    moves[1].wait()
    dim, tgt_count = tgt_ref.shape
    row_count = extra.shape[0]
    lane = iota((TILE, TILE), 1)

    def one_tgt(k, unused):
        block = tgt_ref[:, pl.ds(pl.multiple_of(k * TILE, TILE), TILE)].astype(F32)
        wide = jnp.concatenate([block, jnp.zeros((TILE - dim, TILE), F32)], axis=0).T
        half = -0.5 * jnp.sum(wide * wide, axis=1, keepdims=True)
        a = half.astype(BF16).astype(F32)
        b = (half - a).astype(BF16).astype(F32)
        c = half - a - b
        pieces = jnp.where(lane == dim, a, jnp.where(lane == dim + 1, b, jnp.where(lane == dim + 2, c, 1.0)))
        left[k] = jnp.where(lane < dim, wide, jnp.where(lane < dim + 4, pieces, 0.0)).astype(BF16)
        return unused

    lax.fori_loop(0, tgt_count // TILE, one_tgt, 0)
    line = iota((16, TILE), 0)
    moves[2].wait()

    def one_src(r, unused):
        block = src_ref[:, pl.ds(pl.multiple_of(r * TILE, TILE), TILE)].astype(F32)
        norm = jnp.sum(block * block, axis=0, keepdims=True)
        part_shift = (jnp.sqrt(norm) * (SHIFT / (2.0 * SCALE))).astype(BF16).astype(F32)
        norm_ref[pl.ds(r, 1), :] = norm
        shift_ref[pl.ds(r, 1), :] = part_shift * (2.0 * SCALE)
        extra[r] = jnp.where(line < 3, 1.0, jnp.where(line == 3, -part_shift, 0.0)).astype(BF16)
        return unused

    lax.fori_loop(0, row_count, one_src, 0, unroll=8)
    part[...] = jnp.zeros_like(part)
    for move in moves[3:]:
        move.wait()
    pad = jnp.zeros((TILE - dim - 16, TILE), BF16)

    def step(g, unused):
        base = g * BUILD_UNROLL
        for u in range(BUILD_UNROLL):
            q = base + u
            r = rows_ref[0, q]
            k = tiles_ref[0, q]
            block = src_ref[:, pl.ds(pl.multiple_of(r * TILE, TILE), TILE)]
            right = jnp.concatenate([block, extra[r], pad], axis=0)
            entry = jnp.exp2(dot_n(left[k], right) * (2.0 * SCALE))
            kern_ref[q] = entry.astype(BF16)
            part[pl.ds(q, 1), :] = jnp.sum(entry, axis=0, keepdims=True)
        return unused

    lax.fori_loop(0, pl.cdiv(count_ref[0, 0], BUILD_UNROLL), step, 0)
    sum_ref[...] = sum_slots(by_row_ref[...], part[...])


def in_range(value, low, high):
    return (value >= low) & (value <= high)


def poison(ok, value):
    bad = jnp.max(jnp.where(ok, 0.0, 1.0))
    return jnp.where(bad > 0.0, POISON, value)


def two_rows(table, first, second):
    return jnp.concatenate(
        [
            jnp.broadcast_to(table[pl.ds(first, 1), :], (8, TILE)),
            jnp.broadcast_to(table[pl.ds(second, 1), :], (8, TILE)),
        ],
        axis=0,
    ).astype(BF16)


def start(log_hbm, log_ref, sem, total, table, part):
    move = pltpu.make_async_copy(log_hbm, log_ref, sem)
    move.start()
    part[...] = jnp.zeros_like(part)
    move.wait()
    table[...] = jnp.exp(log_ref[...]) / total


def row_kernel(
    kern_ref, count_ref, tiles_ref, log_hbm, total_ref, by_row_ref, out_ref, table, part, log_ref, sem
):
    total = total_ref[...]
    start(log_hbm, log_ref, sem, total, table, part)

    def step(g, unused):
        base = g * ROW_UNROLL
        for u in range(0, ROW_UNROLL, 2):
            q = base + u
            weights = two_rows(table, tiles_ref[0, q], tiles_ref[0, q + 1])
            pair = jnp.concatenate([kern_ref[q], kern_ref[q + 1]], axis=1)
            got = dot_n(weights, pair)
            part[pl.ds(q, 1), :] = got[0:1, :TILE]
            part[pl.ds(q + 1, 1), :] = got[8:9, TILE:]
        return unused

    lax.fori_loop(0, pl.cdiv(count_ref[0, 0], ROW_UNROLL), step, 0)
    out = sum_slots(by_row_ref[...], part[...])
    out_ref[...] = poison(in_range(total, COL_LOW, COL_HIGH), out)


def col_body(ok, kern_ref, count_ref, rows_ref, total, by_tile_ref, out_ref, table, part, log_hbm, log_ref, sem):
    start(log_hbm, log_ref, sem, total, table, part)
    none = jnp.zeros((16, TILE), BF16)

    def step(g, unused):
        base = g * COL_UNROLL
        for u in range(0, COL_UNROLL, 4):
            q = base + u
            ab = two_rows(table, rows_ref[0, q], rows_ref[0, q + 1])
            cd = two_rows(table, rows_ref[0, q + 2], rows_ref[0, q + 3])
            weights = jnp.concatenate(
                [jnp.concatenate([ab, none], axis=1), jnp.concatenate([none, cd], axis=1)], axis=0
            )
            four = jnp.concatenate(
                [
                    jnp.concatenate([kern_ref[q], kern_ref[q + 2]], axis=1),
                    jnp.concatenate([kern_ref[q + 1], kern_ref[q + 3]], axis=1),
                ],
                axis=0,
            )
            got = dot_t(weights, four)
            part[pl.ds(q, 1), :] = got[0:1, :TILE]
            part[pl.ds(q + 1, 1), :] = got[8:9, TILE:]
            part[pl.ds(q + 2, 1), :] = got[16:17, :TILE]
            part[pl.ds(q + 3, 1), :] = got[24:25, TILE:]
        return unused

    lax.fori_loop(0, pl.cdiv(count_ref[0, 0], COL_UNROLL), step, 0)
    out_ref[...] = poison(ok, sum_slots(by_tile_ref[...], part[...]))


def first_col_kernel(
    kern_ref, count_ref, rows_ref, log_hbm, total_ref, by_tile_ref, out_ref, table, part, log_ref, sem
):
    total = total_ref[...]
    ok = in_range(total, ROW_LOW, ROW_HIGH)
    col_body(ok, kern_ref, count_ref, rows_ref, total, by_tile_ref, out_ref, table, part, log_hbm, log_ref, sem)


def next_col_kernel(
    kern_ref, count_ref, rows_ref, log_hbm, total_ref, earlier_ref, by_tile_ref, out_ref, table, part, log_ref, sem
):
    total = total_ref[...]
    ratio = total / earlier_ref[...]
    ok = in_range(total, ROW_LOW, ROW_HIGH) & in_range(ratio, 1.0 / RATIO, RATIO)
    col_body(ok, kern_ref, count_ref, rows_ref, total, by_tile_ref, out_ref, table, part, log_hbm, log_ref, sem)


def ring_sum(value, axis, size, perm):
    def moved(d):
        return lax.ppermute(value, axis, [(i, perm(i, d)) for i in range(size)])

    opposite, right, left = moved(2), moved(1), moved(3)
    return (value + opposite) + (right + left)


def sum_over_tgt(value):
    value = ring_sum(value, "tgt", 16, lambda i, d: (i // 4) * 4 + (i % 4 + d) % 4)
    return ring_sum(value, "tgt", 16, lambda i, d: (i + 4 * d) % 16)


def sum_over_src(value):
    value = value + lax.ppermute(value, "src", [(i, i ^ 1) for i in range(8)])
    return ring_sum(value, "src", 8, lambda i, d: (i + 2 * d) % 8)


def on_device(source_cells, target_cells, log_source, log_target, support):
    row_count = source_cells.shape[0] // TILE
    tile_count = target_cells.shape[0] // TILE
    cap = 2 * support.size // lax.axis_size("tgt")
    log_rows = log_source.reshape(row_count, TILE)
    log_cols = log_target.reshape(tile_count, TILE)
    array = jax.ShapeDtypeStruct
    kern, total, norm, shift, rows, tiles, count, by_row, by_tile = pl.pallas_call(
        build_kernel,
        out_shape=(
            pltpu.VMEM((cap, TILE, TILE), BF16),
            array((row_count, TILE), F32),
            array((row_count, TILE), F32),
            array((row_count, TILE), F32),
            array((1, cap), jnp.int32),
            array((1, cap), jnp.int32),
            array((1, TILE), jnp.int32),
            array((row_count, cap), BF16),
            array((tile_count, cap), BF16),
        ),
        in_specs=[ANY] * 3,
        out_specs=(VMEM,) * 9,
        scratch_shapes=[
            pltpu.VMEM((tile_count, TILE, TILE), BF16),
            pltpu.VMEM((row_count, 16, TILE), BF16),
            pltpu.VMEM((cap, TILE), F32),
            pltpu.VMEM(support.shape[::-1], jnp.int32),
            pltpu.VMEM(source_cells.shape[::-1], BF16),
            pltpu.VMEM(target_cells.shape[::-1], BF16),
            pltpu.SMEM((1, cap), jnp.int32),
            pltpu.SMEM((1, cap), jnp.int32),
            pltpu.SMEM((1, TILE), jnp.int32),
            pltpu.SemaphoreType.DMA((6,)),
        ],
        compiler_params=params(20),
        name="build",
    )(support.T, source_cells.T, target_cells.T)
    kern = pltpu.with_memory_space_constraint(kern, pltpu.VMEM)

    def call(body, name, slots, log, vmem, out_rows, table_rows):
        return pl.pallas_call(
            body,
            out_shape=array((out_rows, TILE), F32),
            in_specs=[VMEM, SMEM, SMEM, ANY] + [VMEM] * len(vmem),
            out_specs=VMEM,
            scratch_shapes=[
                pltpu.VMEM((table_rows, TILE), F32),
                pltpu.VMEM((cap, TILE), F32),
                pltpu.VMEM((table_rows, TILE), F32),
                pltpu.SemaphoreType.DMA,
            ],
            compiler_params=params(20),
            name=name,
        )(kern, count, slots, log, *vmem)

    first = sum_over_tgt(total)
    cols = call(first_col_kernel, "first_col", rows, log_rows, (first, by_tile), tile_count, row_count)
    cols = sum_over_src(cols)
    second = call(row_kernel, "row", tiles, log_cols, (cols, by_row), row_count, tile_count)
    second = sum_over_tgt(second)
    cols = call(
        next_col_kernel, "next_col", rows, log_rows, (second, first, by_tile), tile_count, row_count
    )
    cols = sum_over_src(cols)
    source_pot = norm + EPS * log_rows - EPS * (jnp.log(second) + LN2 * shift)
    target_pot = EPS * log_cols - EPS * jnp.log(cols)
    return lax.cond(
        jnp.max(cols) < POISONED,
        lambda *unused: (source_pot.reshape(-1), target_pot.reshape(-1)),
        general_path,
        source_cells,
        target_cells,
        log_source,
        log_target,
        support,
    )


def solution(mesh):
    return jax.shard_map(
        on_device,
        mesh=mesh,
        in_specs=(P("src", None), P("tgt", None), P("src"), P("tgt"), P("src", None)),
        out_specs=(P("src"), P("tgt")),
        check_vma=False,
    )
```

```python
import functools

import jax
import jax.numpy as jnp
from jax import lax
from jax.experimental import pallas as pl
from jax.experimental.pallas import tpu as pltpu
from jax.sharding import PartitionSpec as P

TILE = 128
ITERS = 2


EPS = 0.1
NEG = -1e30
HIGH = lax.Precision.HIGHEST

SCALE = 14.426950408889634
LN2 = 0.6931471805599453
SHIFT = 9.0
ROW_LOW = 2.0**-24
ROW_HIGH = 2.0**80
COL_LOW = 2.0**-40
COL_HIGH = 2.0**80
RATIO = 2.0**20
POISON = 3.0e38
POISONED = 1.0e37


def squares_of(tiles):
    values = tiles.astype(jnp.float32)
    return jnp.sum(values * values, axis=2)


def cost_tile(src_block, src_square, tgt_block, tgt_square):
    cross_term = jnp.einsum(
        "bie,bje->bij", src_block, tgt_block, preferred_element_type=jnp.float32
    )
    return src_square[:, :, None] + tgt_square[:, None, :] - 2.0 * cross_term


def one_hot(ids, count):
    return (ids[:, None] == jnp.arange(count, dtype=jnp.int32)[None, :]).astype(jnp.float32)


def pick_rows(selector, table):
    return jnp.dot(selector, table, precision=HIGH, preferred_element_type=jnp.float32)


def fold_block(maxima, totals, selector, block_max, exp_of):
    candidate = jnp.max(jnp.where(selector[:, :, None] > 0.5, block_max[:, None, :], NEG), axis=0)
    new_max = jnp.maximum(maxima, candidate)
    exp_terms = exp_of(pick_rows(selector, new_max))
    added = jnp.dot(selector.T, exp_terms, precision=HIGH, preferred_element_type=jnp.float32)
    return (new_max, totals * jnp.exp(maxima - new_max) + added)


def row_stats(
    slot_rows,
    slot_tiles,
    active,
    pre_src,
    pre_srcn,
    pre_tgt,
    pre_tgtn,
    target_pot,
    row_count,
    num_blocks,
):
    shape_rows = (row_count, pre_srcn.shape[1])
    start_carry = (jnp.full(shape_rows, NEG, jnp.float32), jnp.zeros(shape_rows, jnp.float32))
    tile_count = target_pot.shape[0]

    def row_one_step(carried, block_item):
        maxima, totals = carried
        row_ids, tile_ids, alive, src_block, src_square, tgt_block, tgt_square = block_item
        costs = cost_tile(src_block, src_square, tgt_block, tgt_square)
        slot_pot = pick_rows(one_hot(tile_ids, tile_count), target_pot)
        scores = (slot_pot[:, None, :] - costs) / EPS
        block_max = jnp.where(alive[:, None], jnp.max(scores, axis=2), NEG)
        selector = one_hot(row_ids, row_count) * alive[:, None].astype(jnp.float32)

        def exp_of(slot_max):
            terms = jnp.sum(jnp.exp(scores - slot_max[:, :, None]), axis=2)
            return jnp.where(alive[:, None], terms, 0.0)

        return (fold_block(maxima, totals, selector, block_max, exp_of), None)

    def row_blocks(array):
        return array.reshape((num_blocks, -1) + array.shape[1:])

    block_items = tuple(
        (
            row_blocks(item)
            for item in (slot_rows, slot_tiles, active, pre_src, pre_srcn, pre_tgt, pre_tgtn)
        )
    )
    return lax.scan(row_one_step, start_carry, block_items)[0]


def col_stats(
    slot_rows,
    slot_tiles,
    active,
    pre_src,
    pre_srcn,
    pre_tgt,
    pre_tgtn,
    source_pot,
    tile_count,
    num_blocks,
):
    shape_cols = (tile_count, pre_tgtn.shape[1])
    start_carry = (jnp.full(shape_cols, NEG, jnp.float32), jnp.zeros(shape_cols, jnp.float32))
    row_count = source_pot.shape[0]

    def col_one_step(carried, block_item):
        maxima, totals = carried
        row_ids, tile_ids, alive, src_block, src_square, tgt_block, tgt_square = block_item
        costs = cost_tile(src_block, src_square, tgt_block, tgt_square)
        slot_pot = pick_rows(one_hot(row_ids, row_count), source_pot)
        scores = (slot_pot[:, :, None] - costs) / EPS
        block_max = jnp.where(alive[:, None], jnp.max(scores, axis=1), NEG)
        selector = one_hot(tile_ids, tile_count) * alive[:, None].astype(jnp.float32)

        def exp_of(slot_max):
            terms = jnp.sum(jnp.exp(scores - slot_max[:, None, :]), axis=1)
            return jnp.where(alive[:, None], terms, 0.0)

        return (fold_block(maxima, totals, selector, block_max, exp_of), None)

    def col_blocks(array):
        return array.reshape((num_blocks, -1) + array.shape[1:])

    block_items = tuple(
        (
            col_blocks(item)
            for item in (slot_rows, slot_tiles, active, pre_src, pre_srcn, pre_tgt, pre_tgtn)
        )
    )
    return lax.scan(col_one_step, start_carry, block_items)[0]


def across_targets(maxima, totals):
    highest = lax.pmax(maxima, "tgt")
    return (highest, lax.psum(totals * jnp.exp(maxima - highest), "tgt"))


def across_sources(maxima, totals):
    highest = lax.pmax(maxima, "src")
    return (highest, lax.psum(totals * jnp.exp(maxima - highest), "src"))


def general_path(source_cells, target_cells, log_source, log_target, support):
    row_count = source_cells.shape[0] // TILE
    src_tiles = source_cells.reshape(row_count, TILE, source_cells.shape[1])
    src_norm = squares_of(src_tiles)
    flat_ids = support.reshape(-1)
    num_slots = flat_ids.shape[0]
    tgt_index = lax.axis_index("tgt")
    own_tiles = target_cells.shape[0] // TILE
    per_device = num_slots // lax.axis_size("tgt")
    tgt_tiles = target_cells.reshape(own_tiles, TILE, target_cells.shape[1])
    log_cols = log_target.reshape(own_tiles, TILE)
    capacity = 2 * per_device
    owned = flat_ids // own_tiles == tgt_index
    slot_rank = jnp.cumsum(owned.astype(jnp.int32)) - 1
    target_place = jnp.where(owned, slot_rank, capacity)
    slot_index = (
        jnp.zeros((capacity,), jnp.int32)
        .at[target_place]
        .set(jnp.arange(num_slots, dtype=jnp.int32), mode="drop")
    )
    active = jnp.arange(capacity, dtype=jnp.int32) < jnp.sum(owned.astype(jnp.int32))
    slot_tiles = jnp.clip(flat_ids[slot_index] - tgt_index * own_tiles, 0, own_tiles - 1)
    tgt_norm = squares_of(tgt_tiles)
    tile_count = tgt_tiles.shape[0]
    slot_rows = slot_index // support.shape[1]
    pre_src = src_tiles[slot_rows]
    pre_srcn = src_norm[slot_rows]
    pre_tgt = tgt_tiles[slot_tiles]
    pre_tgtn = tgt_norm[slot_tiles]
    num_blocks = capacity // min(64, capacity)
    log_rows = log_source.reshape(row_count, TILE)
    target_pot = jnp.zeros(log_cols.shape, jnp.float32)
    source_pot = jnp.zeros(log_rows.shape, jnp.float32)
    for iteration in range(ITERS):
        maxima, totals = row_stats(
            slot_rows,
            slot_tiles,
            active,
            pre_src,
            pre_srcn,
            pre_tgt,
            pre_tgtn,
            target_pot,
            row_count,
            num_blocks,
        )
        maxima, totals = across_targets(maxima, totals)
        source_pot = EPS * log_rows - EPS * (maxima + jnp.log(totals))
        maxima, totals = col_stats(
            slot_rows,
            slot_tiles,
            active,
            pre_src,
            pre_srcn,
            pre_tgt,
            pre_tgtn,
            source_pot,
            tile_count,
            num_blocks,
        )
        maxima, totals = across_sources(maxima, totals)
        target_pot = EPS * log_cols - EPS * (maxima + jnp.log(totals))
    return (source_pot.reshape(-1), target_pot.reshape(-1))


CAP_STEP = 128
BUILD_UNROLL = 128
ROW_UNROLL = 128
GROUP = 8
GROUP_UNROLL = 16
SMEM = pl.BlockSpec(memory_space=pltpu.SMEM)
VMEM = pl.BlockSpec(memory_space=pltpu.VMEM)
ANY = pl.BlockSpec(memory_space=pl.ANY)
BF16 = jnp.bfloat16
F32 = jnp.float32


def params(mib):
    return pltpu.CompilerParams(vmem_limit_bytes=mib * 2**20)


def dot_t(a, b):
    return lax.dot_general(a, b, (((1,), (1,)), ((), ())), preferred_element_type=F32)


def dot_n(a, b):
    return jnp.dot(a, b, preferred_element_type=F32)


def ones_where(mask):
    return jnp.where(mask, 1.0, 0.0).astype(BF16)


def iota(shape, axis):
    return lax.broadcasted_iota(jnp.int32, shape, axis)


def list_support(sup_ref, tiles_ref, count_ref, rows_ref, by_row_ref, slots_ref, owners_ref, by_group_ref):
    width, rows = sup_ref.shape
    cap = rows_ref.shape[1]
    own_tiles, groups = by_group_ref.shape
    local = sup_ref[...] - lax.axis_index("tgt") * own_tiles
    owned = (local >= 0) & (local < own_tiles)
    mask = ones_where(owned)
    lower = ones_where(iota((width, width), 1) <= iota((width, width), 0))
    rank = dot_n(lower, mask)
    count = rank[width - 1 : width, :]
    before = ones_where(iota((rows, rows), 1) < iota((rows, rows), 0))
    upto = ones_where(iota((rows, rows), 1) <= iota((rows, rows), 0))
    first = jnp.sum(dot_t(before, mask), axis=1, keepdims=True).astype(jnp.int32)
    last = jnp.sum(dot_t(upto, mask), axis=1, keepdims=True).astype(jnp.int32)
    place = iota((rows, cap), 1)
    by_row = ones_where((first <= place) & (place < last))
    by_row_ref[...] = by_row
    after = ones_where(iota((rows, rows), 0) < iota((rows, rows), 1))
    count8 = jnp.broadcast_to(count, (8, rows)).astype(BF16)
    first8 = dot_n(count8, after)
    high = jnp.floor(first8 * (1.0 / 32.0))
    low = first8 - 32.0 * high
    row_id = iota((8, rows), 1).astype(F32)
    tile = jnp.where(owned, local, 0).astype(F32)
    table = jnp.concatenate([tile, jnp.where(owned, rank, 0.0), row_id, high, low], axis=0)
    got = dot_n(table.astype(BF16), by_row)
    begin = 32.0 * got[2 * width + 8 : 2 * width + 9] + got[2 * width + 16 : 2 * width + 17]
    place_f = iota((1, cap), 1).astype(F32)
    want = place_f - begin + 1.0
    tiles = jnp.sum(jnp.where(got[width : 2 * width] == want, got[:width], 0.0), axis=0, keepdims=True)
    tiles_ref[...] = tiles.astype(jnp.int32)
    rows_ref[...] = got[2 * width : 2 * width + 1].astype(jnp.int32)
    total = jnp.sum(count, axis=1, keepdims=True)
    held = (iota((own_tiles, cap), 0).astype(F32) == tiles) & (place_f < total)
    by_tile = ones_where(held)
    member = dot_t(by_row, by_tile)
    rank = jnp.where(member > 0.5, dot_n(before, member.astype(BF16)), 384.0).astype(BF16)
    place_high = jnp.floor(place_f * (1.0 / 32.0))
    slot_high = dot_t(by_row * place_high.astype(BF16), by_tile).astype(BF16)
    slot_low = dot_t(by_row * (place_f - 32.0 * place_high).astype(BF16), by_tile).astype(BF16)
    held_count = jnp.sum(jnp.where(held, 1.0, 0.0), axis=1, keepdims=True)
    group_count = jnp.floor((held_count + (GROUP - 1.0)) * (1.0 / GROUP))
    earlier = ones_where(iota((own_tiles, own_tiles), 1) < iota((own_tiles, own_tiles), 0))
    group_wide = jnp.broadcast_to(group_count, (own_tiles, TILE)).astype(BF16)
    begin = dot_n(earlier, group_wide)[:, :1]
    group = iota((own_tiles, groups), 1).astype(F32)
    by_group_ref[...] = ones_where((begin <= group) & (group < begin + group_count))
    spots = groups * GROUP
    spot = iota((own_tiles, spots), 1).astype(F32) - GROUP * begin
    inside = (spot >= 0.0) & (spot < held_count)
    by_spot = ones_where(inside)
    wanted = jnp.sum(jnp.where(inside, spot, 0.0), axis=0, keepdims=True)
    filled = jnp.sum(jnp.where(inside, 1.0, 0.0), axis=0, keepdims=True)
    match = (dot_n(rank, by_spot) == wanted) & (filled > 0.5)
    slot = 32.0 * dot_n(slot_high, by_spot) + dot_n(slot_low, by_spot)
    slots_ref[...] = jnp.sum(jnp.where(match, slot, 0.0), axis=0, keepdims=True).astype(jnp.int32)
    row_of = iota((rows, spots), 0).astype(F32)
    owner = jnp.sum(jnp.where(match, row_of, 0.0), axis=0, keepdims=True)
    owners_ref[...] = jnp.where(filled > 0.5, owner, float(rows)).astype(jnp.int32)
    all_groups = jnp.sum(group_count, axis=0, keepdims=True)
    lane = iota(count_ref.shape, 1)
    count_ref[...] = jnp.where(lane == 0, total, all_groups).astype(jnp.int32)


def sum_slots(members, parts):
    high = parts.astype(BF16)
    low = (parts - high.astype(F32)).astype(BF16)
    return dot_n(members, high) + dot_n(members, low)


def build_kernel(
    sup_hbm, src_hbm, tgt_hbm,
    kern_ref, sum_ref, norm_ref, shift_ref, tiles_out, count_out, by_row_ref, slots_ref, owners_ref, by_group_ref,
    left, minus, part, rows_out, sup_ref, src_ref, tgt_ref, rows_ref, tiles_ref, count_ref, sems,
):
    moves = [
        pltpu.make_async_copy(*pair, sems.at[i])
        for i, pair in enumerate(
            [
                (sup_hbm, sup_ref),
                (tgt_hbm, tgt_ref),
                (src_hbm, src_ref),
                (rows_out, rows_ref),
                (tiles_out, tiles_ref),
                (count_out, count_ref),
            ]
        )
    ]
    for move in moves[:3]:
        move.start()
    moves[0].wait()
    list_support(sup_ref, tiles_out, count_out, rows_out, by_row_ref, slots_ref, owners_ref, by_group_ref)
    for move in moves[3:]:
        move.start()
    moves[1].wait()
    dim, tgt_count = tgt_ref.shape
    def one_tgt(k, unused):
        block = tgt_ref[:, pl.ds(pl.multiple_of(k * TILE, TILE), TILE)].astype(F32)
        half = -0.5 * jnp.sum(block * block, axis=0, keepdims=True)
        first = half.astype(BF16).astype(F32)
        second = (half - first).astype(BF16).astype(F32)
        third = half - first - second
        line = iota((8, TILE), 0)
        extra = jnp.where(line == 0, first, jnp.where(line == 1, second, jnp.where(line == 2, third, 1.0)))
        extra = jnp.where(line < 4, extra, 0.0)
        none = jnp.zeros((TILE - dim - 8, TILE), F32)
        left[k] = jnp.concatenate([block, extra, none], axis=0).T.astype(BF16)
        return unused

    lax.fori_loop(0, tgt_count // TILE, one_tgt, 0, unroll=8)
    moves[2].wait()

    def eight_src(g, unused):
        norms = []
        for u in range(8):
            at = pl.multiple_of((g * 8 + u) * TILE, TILE)
            block = src_ref[:, pl.ds(at, TILE)].astype(F32)
            norms.append(jnp.sum(block * block, axis=0, keepdims=True))
        norm = jnp.concatenate(norms, axis=0)
        at = pl.multiple_of(g * 8, 8)
        norm_ref[pl.ds(at, 8), :] = norm
        part_shift = (jnp.sqrt(norm) * (SHIFT / (2.0 * SCALE))).astype(BF16).astype(F32)
        minus[pl.ds(at, 8), :] = -part_shift
        shift_ref[pl.ds(at, 8), :] = part_shift * (2.0 * SCALE)
        return unused

    lax.fori_loop(0, norm_ref.shape[0] // 8, eight_src, 0, unroll=2)
    part[...] = jnp.zeros_like(part)
    for move in moves[3:]:
        move.wait()
    line = iota((16, TILE), 0)
    pad = jnp.zeros((TILE - dim - 16, TILE), BF16)
    none = jnp.zeros((TILE, TILE), BF16)

    def right_of(q):
        r = rows_ref[0, q]
        block = src_ref[:, pl.ds(pl.multiple_of(r * TILE, TILE), TILE)]
        extra = jnp.where(line < 3, 1.0, jnp.where(line == 3, minus[pl.ds(r, 1), :], 0.0)).astype(BF16)
        return jnp.concatenate([block, extra, pad], axis=0)

    def step(g, unused):
        base = g * BUILD_UNROLL
        for u in range(0, BUILD_UNROLL, 2):
            q = base + u
            lefts = jnp.concatenate([left[tiles_ref[0, q]], left[tiles_ref[0, q + 1]]], axis=1)
            rights = jnp.concatenate(
                [
                    jnp.concatenate([right_of(q), none], axis=0),
                    jnp.concatenate([none, right_of(q + 1)], axis=0),
                ],
                axis=1,
            )
            entry = jnp.exp2(dot_n(lefts, rights) * (2.0 * SCALE))
            kern_ref[q] = entry[:, :TILE].astype(BF16)
            kern_ref[q + 1] = entry[:, TILE:].astype(BF16)
            sums = jnp.sum(entry, axis=0, keepdims=True)
            part[pl.ds(q, 1), :] = sums[:, :TILE]
            part[pl.ds(q + 1, 1), :] = sums[:, TILE:]
        return unused

    lax.fori_loop(0, pl.cdiv(count_ref[0, 0], BUILD_UNROLL), step, 0)
    sum_ref[...] = sum_slots(by_row_ref[...], part[...])


def in_range(value, low, high):
    return (value >= low) & (value <= high)


def poison(ok, value):
    bad = jnp.max(jnp.where(ok, 0.0, 1.0))
    return jnp.where(bad > 0.0, POISON, value)


def two_rows(table, first, second):
    return jnp.concatenate(
        [
            jnp.broadcast_to(table[pl.ds(first, 1), :], (8, TILE)),
            jnp.broadcast_to(table[pl.ds(second, 1), :], (8, TILE)),
        ],
        axis=0,
    ).astype(BF16)


def start(log_hbm, log_ref, sem, total, table, part):
    move = pltpu.make_async_copy(log_hbm, log_ref, sem)
    move.start()
    part[...] = jnp.zeros_like(part)
    move.wait()
    table[...] = jnp.exp(log_ref[...]) / total


def row_kernel(
    kern_ref, count_ref, tiles_ref, log_hbm, total_ref, by_row_ref, out_ref, table, part, log_ref, sem
):
    total = total_ref[...]
    start(log_hbm, log_ref, sem, total, table.at[pl.ds(0, total.shape[0])], part)

    def step(g, unused):
        base = g * ROW_UNROLL
        for u in range(0, ROW_UNROLL, 2):
            q = base + u
            weights = two_rows(table, tiles_ref[0, q], tiles_ref[0, q + 1])
            pair = jnp.concatenate([kern_ref[q], kern_ref[q + 1]], axis=1)
            got = dot_n(weights, pair)
            part[pl.ds(q, 1), :] = got[0:1, :TILE]
            part[pl.ds(q + 1, 1), :] = got[8:9, TILE:]
        return unused

    lax.fori_loop(0, pl.cdiv(count_ref[0, 0], ROW_UNROLL), step, 0)
    out = sum_slots(by_row_ref[...], part[...])
    out_ref[...] = poison(in_range(total, COL_LOW, COL_HIGH), out)


def col_body(ok, kern_ref, count_ref, slots_ref, owners_ref, total, by_group_ref, out_ref, table, part, log_hbm, log_ref, sem):
    rows = total.shape[0]
    table[pl.ds(rows, 8), :] = jnp.zeros((8, TILE), F32)
    start(log_hbm, log_ref, sem, total, table.at[pl.ds(0, rows)], part)
    ones = jnp.ones((16, TILE), BF16)

    def weighed(spot):
        weight = jnp.broadcast_to(table[pl.ds(owners_ref[0, spot], 1), :], (16, TILE)).astype(BF16)
        return kern_ref[slots_ref[0, spot]] * jnp.concatenate([weight] * (TILE // 16), axis=0)

    def group_sum(g):
        terms = [weighed(g * GROUP + i) for i in range(GROUP)]
        while len(terms) > 1:
            terms = [a + b for a, b in zip(terms[::2], terms[1::2], strict=True)]
        return terms[0]

    def step(i, unused):
        base = i * GROUP_UNROLL
        for u in range(0, GROUP_UNROLL, 2):
            g = base + u
            got = dot_t(ones, jnp.concatenate([group_sum(g), group_sum(g + 1)], axis=0))
            part[pl.ds(g, 1), :] = got[0:1, :TILE]
            part[pl.ds(g + 1, 1), :] = got[0:1, TILE:]
        return unused

    lax.fori_loop(0, pl.cdiv(count_ref[0, 1], GROUP_UNROLL), step, 0)
    out_ref[...] = poison(ok, sum_slots(by_group_ref[...], part[...]))


def first_col_kernel(
    kern_ref, count_ref, slots_ref, owners_ref, log_hbm, total_ref, by_group_ref, out_ref, table, part, log_ref, sem
):
    total = total_ref[...]
    ok = in_range(total, ROW_LOW, ROW_HIGH)
    col_body(
        ok, kern_ref, count_ref, slots_ref, owners_ref, total, by_group_ref, out_ref, table, part, log_hbm, log_ref, sem
    )


def next_col_kernel(
    kern_ref, count_ref, slots_ref, owners_ref, log_hbm, total_ref, earlier_ref, by_group_ref, out_ref,
    table, part, log_ref, sem,
):
    total = total_ref[...]
    ratio = total / earlier_ref[...]
    ok = in_range(total, ROW_LOW, ROW_HIGH) & in_range(ratio, 1.0 / RATIO, RATIO)
    col_body(
        ok, kern_ref, count_ref, slots_ref, owners_ref, total, by_group_ref, out_ref, table, part, log_hbm, log_ref, sem
    )


def ring_sum(value, axis, size, perm):
    def moved(d):
        return lax.ppermute(value, axis, [(i, perm(i, d)) for i in range(size)])

    opposite, right, left = moved(2), moved(1), moved(3)
    return (value + opposite) + (right + left)


def sum_over_tgt(value):
    value = ring_sum(value, "tgt", 16, lambda i, d: (i // 4) * 4 + (i % 4 + d) % 4)
    return ring_sum(value, "tgt", 16, lambda i, d: (i + 4 * d) % 16)


def sum_over_src(value):
    value = value + lax.ppermute(value, "src", [(i, i ^ 1) for i in range(8)])
    return ring_sum(value, "src", 8, lambda i, d: (i + 2 * d) % 8)


def on_device(source_cells, target_cells, log_source, log_target, support):
    row_count = source_cells.shape[0] // TILE
    tile_count = target_cells.shape[0] // TILE
    cap = 2 * support.size // lax.axis_size("tgt")
    log_rows = log_source.reshape(row_count, TILE)
    log_cols = log_target.reshape(tile_count, TILE)
    array = jax.ShapeDtypeStruct
    groups = -(-(cap // GROUP + tile_count) // GROUP_UNROLL) * GROUP_UNROLL
    kern, total, norm, shift, tiles, count, by_row, slots, owners, by_group = pl.pallas_call(
        build_kernel,
        out_shape=(
            pltpu.VMEM((cap, TILE, TILE), BF16),
            array((row_count, TILE), F32),
            array((row_count, TILE), F32),
            array((row_count, TILE), F32),
            array((1, cap), jnp.int32),
            array((1, TILE), jnp.int32),
            array((row_count, cap), BF16),
            array((1, groups * GROUP), jnp.int32),
            array((1, groups * GROUP), jnp.int32),
            array((tile_count, groups), BF16),
        ),
        in_specs=[ANY] * 3,
        out_specs=(VMEM,) * 10,
        scratch_shapes=[
            pltpu.VMEM((tile_count, TILE, TILE), BF16),
            pltpu.VMEM((row_count, TILE), F32),
            pltpu.VMEM((cap, TILE), F32),
            pltpu.VMEM((1, cap), jnp.int32),
            pltpu.VMEM(support.shape[::-1], jnp.int32),
            pltpu.VMEM(source_cells.shape[::-1], BF16),
            pltpu.VMEM(target_cells.shape[::-1], BF16),
            pltpu.SMEM((1, cap), jnp.int32),
            pltpu.SMEM((1, cap), jnp.int32),
            pltpu.SMEM((1, TILE), jnp.int32),
            pltpu.SemaphoreType.DMA((6,)),
        ],
        compiler_params=params(20),
        name="build",
    )(support.T, source_cells.T, target_cells.T)
    kern = pltpu.with_memory_space_constraint(kern, pltpu.VMEM)

    def call(body, name, lists, log, vmem, out_rows, parts):
        return pl.pallas_call(
            body,
            out_shape=array((out_rows, TILE), F32),
            in_specs=[VMEM] + [SMEM] * (1 + len(lists)) + [ANY] + [VMEM] * len(vmem),
            out_specs=VMEM,
            scratch_shapes=[
                pltpu.VMEM((log.shape[0] + 8, TILE), F32),
                pltpu.VMEM((parts, TILE), F32),
                pltpu.VMEM(log.shape, F32),
                pltpu.SemaphoreType.DMA,
            ],
            compiler_params=params(20),
            name=name,
        )(kern, count, *lists, log, *vmem)

    def cols_of(body, name, totals):
        return sum_over_src(
            call(body, name, (slots, owners), log_rows, (*totals, by_group), tile_count, groups)
        )

    first = sum_over_tgt(total)
    cols = cols_of(first_col_kernel, "first_col", (first,))
    second = sum_over_tgt(call(row_kernel, "row", (tiles,), log_cols, (cols, by_row), row_count, cap))
    cols = cols_of(next_col_kernel, "next_col", (second, first))
    source_pot = norm + EPS * log_rows - EPS * (jnp.log(second) + LN2 * shift)
    target_pot = EPS * log_cols - EPS * jnp.log(cols)
    return lax.cond(
        jnp.max(cols) < POISONED,
        lambda *unused: (source_pot.reshape(-1), target_pot.reshape(-1)),
        general_path,
        source_cells,
        target_cells,
        log_source,
        log_target,
        support,
    )


def solution(mesh):
    return jax.shard_map(
        on_device,
        mesh=mesh,
        in_specs=(P("src", None), P("tgt", None), P("src"), P("tgt"), P("src", None)),
        out_specs=(P("src"), P("tgt")),
        check_vma=False,
    )
```

```python
import functools

import jax
import jax.numpy as jnp
from jax import lax
from jax.experimental import pallas as pl
from jax.experimental.pallas import tpu as pltpu
from jax.sharding import PartitionSpec as P

TILE = 128
ITERS = 2


EPS = 0.1
NEG = -1e30
HIGH = lax.Precision.HIGHEST

SCALE = 14.426950408889634
LN2 = 0.6931471805599453
SHIFT = 9.0
ROW_LOW = 2.0**-24
ROW_HIGH = 2.0**80
COL_LOW = 2.0**-40
COL_HIGH = 2.0**80
RATIO = 2.0**20
POISON = 3.0e38
POISONED = 1.0e37


def squares_of(tiles):
    values = tiles.astype(jnp.float32)
    return jnp.sum(values * values, axis=2)


def cost_tile(src_block, src_square, tgt_block, tgt_square):
    cross_term = jnp.einsum(
        "bie,bje->bij", src_block, tgt_block, preferred_element_type=jnp.float32
    )
    return src_square[:, :, None] + tgt_square[:, None, :] - 2.0 * cross_term


def one_hot(ids, count):
    return (ids[:, None] == jnp.arange(count, dtype=jnp.int32)[None, :]).astype(jnp.float32)


def pick_rows(selector, table):
    return jnp.dot(selector, table, precision=HIGH, preferred_element_type=jnp.float32)


def fold_block(maxima, totals, selector, block_max, exp_of):
    candidate = jnp.max(jnp.where(selector[:, :, None] > 0.5, block_max[:, None, :], NEG), axis=0)
    new_max = jnp.maximum(maxima, candidate)
    exp_terms = exp_of(pick_rows(selector, new_max))
    added = jnp.dot(selector.T, exp_terms, precision=HIGH, preferred_element_type=jnp.float32)
    return (new_max, totals * jnp.exp(maxima - new_max) + added)


def row_stats(
    slot_rows,
    slot_tiles,
    active,
    pre_src,
    pre_srcn,
    pre_tgt,
    pre_tgtn,
    target_pot,
    row_count,
    num_blocks,
):
    shape_rows = (row_count, pre_srcn.shape[1])
    start_carry = (jnp.full(shape_rows, NEG, jnp.float32), jnp.zeros(shape_rows, jnp.float32))
    tile_count = target_pot.shape[0]

    def row_one_step(carried, block_item):
        maxima, totals = carried
        row_ids, tile_ids, alive, src_block, src_square, tgt_block, tgt_square = block_item
        costs = cost_tile(src_block, src_square, tgt_block, tgt_square)
        slot_pot = pick_rows(one_hot(tile_ids, tile_count), target_pot)
        scores = (slot_pot[:, None, :] - costs) / EPS
        block_max = jnp.where(alive[:, None], jnp.max(scores, axis=2), NEG)
        selector = one_hot(row_ids, row_count) * alive[:, None].astype(jnp.float32)

        def exp_of(slot_max):
            terms = jnp.sum(jnp.exp(scores - slot_max[:, :, None]), axis=2)
            return jnp.where(alive[:, None], terms, 0.0)

        return (fold_block(maxima, totals, selector, block_max, exp_of), None)

    def row_blocks(array):
        return array.reshape((num_blocks, -1) + array.shape[1:])

    block_items = tuple(
        (
            row_blocks(item)
            for item in (slot_rows, slot_tiles, active, pre_src, pre_srcn, pre_tgt, pre_tgtn)
        )
    )
    return lax.scan(row_one_step, start_carry, block_items)[0]


def col_stats(
    slot_rows,
    slot_tiles,
    active,
    pre_src,
    pre_srcn,
    pre_tgt,
    pre_tgtn,
    source_pot,
    tile_count,
    num_blocks,
):
    shape_cols = (tile_count, pre_tgtn.shape[1])
    start_carry = (jnp.full(shape_cols, NEG, jnp.float32), jnp.zeros(shape_cols, jnp.float32))
    row_count = source_pot.shape[0]

    def col_one_step(carried, block_item):
        maxima, totals = carried
        row_ids, tile_ids, alive, src_block, src_square, tgt_block, tgt_square = block_item
        costs = cost_tile(src_block, src_square, tgt_block, tgt_square)
        slot_pot = pick_rows(one_hot(row_ids, row_count), source_pot)
        scores = (slot_pot[:, :, None] - costs) / EPS
        block_max = jnp.where(alive[:, None], jnp.max(scores, axis=1), NEG)
        selector = one_hot(tile_ids, tile_count) * alive[:, None].astype(jnp.float32)

        def exp_of(slot_max):
            terms = jnp.sum(jnp.exp(scores - slot_max[:, None, :]), axis=1)
            return jnp.where(alive[:, None], terms, 0.0)

        return (fold_block(maxima, totals, selector, block_max, exp_of), None)

    def col_blocks(array):
        return array.reshape((num_blocks, -1) + array.shape[1:])

    block_items = tuple(
        (
            col_blocks(item)
            for item in (slot_rows, slot_tiles, active, pre_src, pre_srcn, pre_tgt, pre_tgtn)
        )
    )
    return lax.scan(col_one_step, start_carry, block_items)[0]


def across_targets(maxima, totals):
    highest = lax.pmax(maxima, "tgt")
    return (highest, lax.psum(totals * jnp.exp(maxima - highest), "tgt"))


def across_sources(maxima, totals):
    highest = lax.pmax(maxima, "src")
    return (highest, lax.psum(totals * jnp.exp(maxima - highest), "src"))


def general_path(source_cells, target_cells, log_source, log_target, support):
    row_count = source_cells.shape[0] // TILE
    src_tiles = source_cells.reshape(row_count, TILE, source_cells.shape[1])
    src_norm = squares_of(src_tiles)
    flat_ids = support.reshape(-1)
    num_slots = flat_ids.shape[0]
    tgt_index = lax.axis_index("tgt")
    own_tiles = target_cells.shape[0] // TILE
    per_device = num_slots // lax.axis_size("tgt")
    tgt_tiles = target_cells.reshape(own_tiles, TILE, target_cells.shape[1])
    log_cols = log_target.reshape(own_tiles, TILE)
    capacity = 2 * per_device
    owned = flat_ids // own_tiles == tgt_index
    slot_rank = jnp.cumsum(owned.astype(jnp.int32)) - 1
    target_place = jnp.where(owned, slot_rank, capacity)
    slot_index = (
        jnp.zeros((capacity,), jnp.int32)
        .at[target_place]
        .set(jnp.arange(num_slots, dtype=jnp.int32), mode="drop")
    )
    active = jnp.arange(capacity, dtype=jnp.int32) < jnp.sum(owned.astype(jnp.int32))
    slot_tiles = jnp.clip(flat_ids[slot_index] - tgt_index * own_tiles, 0, own_tiles - 1)
    tgt_norm = squares_of(tgt_tiles)
    tile_count = tgt_tiles.shape[0]
    slot_rows = slot_index // support.shape[1]
    pre_src = src_tiles[slot_rows]
    pre_srcn = src_norm[slot_rows]
    pre_tgt = tgt_tiles[slot_tiles]
    pre_tgtn = tgt_norm[slot_tiles]
    num_blocks = capacity // min(64, capacity)
    log_rows = log_source.reshape(row_count, TILE)
    target_pot = jnp.zeros(log_cols.shape, jnp.float32)
    source_pot = jnp.zeros(log_rows.shape, jnp.float32)
    for iteration in range(ITERS):
        maxima, totals = row_stats(
            slot_rows,
            slot_tiles,
            active,
            pre_src,
            pre_srcn,
            pre_tgt,
            pre_tgtn,
            target_pot,
            row_count,
            num_blocks,
        )
        maxima, totals = across_targets(maxima, totals)
        source_pot = EPS * log_rows - EPS * (maxima + jnp.log(totals))
        maxima, totals = col_stats(
            slot_rows,
            slot_tiles,
            active,
            pre_src,
            pre_srcn,
            pre_tgt,
            pre_tgtn,
            source_pot,
            tile_count,
            num_blocks,
        )
        maxima, totals = across_sources(maxima, totals)
        target_pot = EPS * log_cols - EPS * (maxima + jnp.log(totals))
    return (source_pot.reshape(-1), target_pot.reshape(-1))


CAP_STEP = 128
BUILD_UNROLL = 256
ROW_UNROLL = 256
GROUP = 8
GROUP_UNROLL = 32
SMEM = pl.BlockSpec(memory_space=pltpu.SMEM)
VMEM = pl.BlockSpec(memory_space=pltpu.VMEM)
ANY = pl.BlockSpec(memory_space=pl.ANY)
BF16 = jnp.bfloat16
F32 = jnp.float32


def params(mib):
    return pltpu.CompilerParams(vmem_limit_bytes=mib * 2**20)


def dot_t(a, b):
    return lax.dot_general(a, b, (((1,), (1,)), ((), ())), preferred_element_type=F32)


def dot_n(a, b):
    return jnp.dot(a, b, preferred_element_type=F32)


def ones_where(mask):
    return jnp.where(mask, 1.0, 0.0).astype(BF16)


def iota(shape, axis):
    return lax.broadcasted_iota(jnp.int32, shape, axis)


def strictly_before(size):
    return ones_where(iota((size, size), 1) < iota((size, size), 0))


def list_support(sup_ref, tiles_ref, count_ref, rows_ref, by_row_ref, own_tiles):
    width, rows = sup_ref.shape
    cap = rows_ref.shape[1]
    local = sup_ref[...] - lax.axis_index("tgt") * own_tiles
    owned = (local >= 0) & (local < own_tiles)
    mask = ones_where(owned)
    lower = ones_where(iota((width, width), 1) <= iota((width, width), 0))
    rank = dot_n(lower, mask)
    count = rank[width - 1 : width, :]
    upto = ones_where(iota((rows, rows), 1) <= iota((rows, rows), 0))
    first = jnp.sum(dot_t(strictly_before(rows), mask), axis=1, keepdims=True).astype(jnp.int32)
    last = jnp.sum(dot_t(upto, mask), axis=1, keepdims=True).astype(jnp.int32)
    place = iota((rows, cap), 1)
    by_row = ones_where((first <= place) & (place < last))
    by_row_ref[...] = by_row
    after = ones_where(iota((rows, rows), 0) < iota((rows, rows), 1))
    count8 = jnp.broadcast_to(count, (8, rows)).astype(BF16)
    first8 = dot_n(count8, after)
    high = jnp.floor(first8 * (1.0 / 32.0))
    low = first8 - 32.0 * high
    row_id = iota((8, rows), 1).astype(F32)
    tile = jnp.where(owned, local, 0).astype(F32)
    table = jnp.concatenate([tile, jnp.where(owned, rank, 0.0), row_id, high, low], axis=0)
    got = dot_n(table.astype(BF16), by_row)
    begin = 32.0 * got[2 * width + 8 : 2 * width + 9] + got[2 * width + 16 : 2 * width + 17]
    want = iota((1, cap), 1).astype(F32) - begin + 1.0
    tiles = jnp.sum(jnp.where(got[width : 2 * width] == want, got[:width], 0.0), axis=0, keepdims=True)
    tiles_ref[...] = tiles.astype(jnp.int32)
    rows_ref[...] = got[2 * width : 2 * width + 1].astype(jnp.int32)
    total = jnp.sum(count, axis=1, keepdims=True)
    count_ref[...] = jnp.broadcast_to(total, count_ref.shape).astype(jnp.int32)


def group_kernel(tiles_ref, count_ref, by_row_ref, slots_ref, owners_ref, by_group_ref, group_count_ref):
    rows, cap = by_row_ref.shape
    own_tiles, groups = by_group_ref.shape
    by_row = by_row_ref[...]
    place = iota((1, cap), 1)
    held = (iota((own_tiles, cap), 0) == tiles_ref[...]) & (place < count_ref[:, :1])
    place_f = place.astype(F32)
    by_tile = ones_where(held)
    member = dot_t(by_row, by_tile)
    rank = jnp.where(member > 0.5, dot_n(strictly_before(rows), member.astype(BF16)), 384.0).astype(BF16)
    place_high = jnp.floor(place_f * (1.0 / 32.0))
    slot_high = dot_t(by_row * place_high.astype(BF16), by_tile).astype(BF16)
    slot_low = dot_t(by_row * (place_f - 32.0 * place_high).astype(BF16), by_tile).astype(BF16)
    held_count = jnp.sum(jnp.where(held, 1.0, 0.0), axis=1, keepdims=True)
    group_count = jnp.floor((held_count + (GROUP - 1.0)) * (1.0 / GROUP))
    group_wide = jnp.broadcast_to(group_count, (own_tiles, TILE)).astype(BF16)
    begin = dot_n(strictly_before(own_tiles), group_wide)[:, :1]
    group = iota((own_tiles, groups), 1).astype(F32)
    by_group_ref[...] = ones_where((begin <= group) & (group < begin + group_count))
    spots = groups * GROUP
    spot = iota((own_tiles, spots), 1).astype(F32) - GROUP * begin
    inside = (spot >= 0.0) & (spot < held_count)
    by_spot = ones_where(inside)
    wanted = jnp.sum(jnp.where(inside, spot, 0.0), axis=0, keepdims=True)
    filled = jnp.sum(jnp.where(inside, 1.0, 0.0), axis=0, keepdims=True)
    match = (dot_n(rank, by_spot) == wanted) & (filled > 0.5)
    slot = 32.0 * dot_n(slot_high, by_spot) + dot_n(slot_low, by_spot)
    slots_ref[...] = jnp.sum(jnp.where(match, slot, 0.0), axis=0, keepdims=True).astype(jnp.int32)
    row_of = iota((rows, spots), 0).astype(F32)
    owner = jnp.sum(jnp.where(match, row_of, 0.0), axis=0, keepdims=True)
    owners_ref[...] = jnp.where(filled > 0.5, owner, float(rows)).astype(jnp.int32)
    all_groups = jnp.sum(group_count, axis=0, keepdims=True)
    group_count_ref[...] = jnp.broadcast_to(all_groups, group_count_ref.shape).astype(jnp.int32)


def sum_slots(members, parts):
    high = parts.astype(BF16)
    low = (parts - high.astype(F32)).astype(BF16)
    return dot_n(members, high) + dot_n(members, low)


def build_kernel(
    sup_hbm, src_hbm, tgt_hbm, log_rows_hbm, log_cols_hbm,
    kern_ref, sum_ref, norm_ref, shift_ref, mass_rows_ref, mass_cols_ref, tiles_out, count_out, by_row_ref,
    left, minus, part, rows_out, sup_ref, src_ref, tgt_ref, rows_ref, tiles_ref, count_ref, sems,
):
    moves = [
        pltpu.make_async_copy(*pair, sems.at[i])
        for i, pair in enumerate(
            [
                (sup_hbm, sup_ref),
                (tgt_hbm, tgt_ref),
                (src_hbm, src_ref),
                (log_rows_hbm, mass_rows_ref),
                (log_cols_hbm, mass_cols_ref),
                (rows_out, rows_ref),
                (tiles_out, tiles_ref),
                (count_out, count_ref),
            ]
        )
    ]
    for move in moves[:5]:
        move.start()
    moves[0].wait()
    dim, tgt_count = tgt_ref.shape
    list_support(sup_ref, tiles_out, count_out, rows_out, by_row_ref, tgt_count // TILE)
    for move in moves[5:]:
        move.start()
    moves[1].wait()

    def one_tgt(k, unused):
        block = tgt_ref[:, pl.ds(pl.multiple_of(k * TILE, TILE), TILE)].astype(F32)
        half = -0.5 * jnp.sum(block * block, axis=0, keepdims=True)
        first = half.astype(BF16).astype(F32)
        second = (half - first).astype(BF16).astype(F32)
        third = half - first - second
        line = iota((8, TILE), 0)
        extra = jnp.where(line == 0, first, jnp.where(line == 1, second, jnp.where(line == 2, third, 1.0)))
        extra = jnp.where(line < 4, extra, 0.0)
        none = jnp.zeros((TILE - dim - 8, TILE), F32)
        left[k] = jnp.concatenate([block, extra, none], axis=0).T.astype(BF16)
        return unused

    lax.fori_loop(0, tgt_count // TILE, one_tgt, 0, unroll=8)
    moves[2].wait()

    def eight_src(g, unused):
        norms = []
        for u in range(8):
            at = pl.multiple_of((g * 8 + u) * TILE, TILE)
            block = src_ref[:, pl.ds(at, TILE)].astype(F32)
            norms.append(jnp.sum(block * block, axis=0, keepdims=True))
        norm = jnp.concatenate(norms, axis=0)
        at = pl.multiple_of(g * 8, 8)
        norm_ref[pl.ds(at, 8), :] = norm
        part_shift = (jnp.sqrt(norm) * (SHIFT / (2.0 * SCALE))).astype(BF16).astype(F32)
        minus[pl.ds(at, 8), :] = -part_shift
        shift_ref[pl.ds(at, 8), :] = part_shift * (2.0 * SCALE)
        return unused

    lax.fori_loop(0, norm_ref.shape[0] // 8, eight_src, 0, unroll=2)
    part[...] = jnp.zeros_like(part)
    for move in moves[3:]:
        move.wait()
    mass_rows_ref[...] = jnp.exp(mass_rows_ref[...])
    mass_cols_ref[...] = jnp.exp(mass_cols_ref[...])
    line = iota((16, TILE), 0)
    pad = jnp.zeros((TILE - dim - 16, TILE), BF16)
    none = jnp.zeros((TILE, TILE), BF16)

    def right_of(q):
        r = rows_ref[0, q]
        block = src_ref[:, pl.ds(pl.multiple_of(r * TILE, TILE), TILE)]
        extra = jnp.where(line < 3, 1.0, jnp.where(line == 3, minus[pl.ds(r, 1), :], 0.0)).astype(BF16)
        return jnp.concatenate([block, extra, pad], axis=0)

    def step(g, unused):
        base = g * BUILD_UNROLL
        for u in range(0, BUILD_UNROLL, 2):
            q = base + u
            lefts = jnp.concatenate([left[tiles_ref[0, q]], left[tiles_ref[0, q + 1]]], axis=1)
            rights = jnp.concatenate(
                [
                    jnp.concatenate([right_of(q), none], axis=0),
                    jnp.concatenate([none, right_of(q + 1)], axis=0),
                ],
                axis=1,
            )
            entry = jnp.exp2(dot_n(lefts, rights) * (2.0 * SCALE))
            kern_ref[q] = entry[:, :TILE].astype(BF16)
            kern_ref[q + 1] = entry[:, TILE:].astype(BF16)
            sums = jnp.sum(entry, axis=0, keepdims=True)
            part[pl.ds(q, 1), :] = sums[:, :TILE]
            part[pl.ds(q + 1, 1), :] = sums[:, TILE:]
        return unused

    lax.fori_loop(0, pl.cdiv(count_ref[0, 0], BUILD_UNROLL), step, 0)
    sum_ref[...] = sum_slots(by_row_ref[...], part[...]).astype(BF16)


def in_range(value, low, high):
    return (value >= low) & (value <= high)


def poison(ok, value):
    bad = jnp.max(jnp.where(ok, 0.0, 1.0))
    return jnp.where(bad > 0.0, POISON, value)


def two_rows(table, first, second):
    return jnp.concatenate(
        [
            jnp.broadcast_to(table[pl.ds(first, 1), :], (8, TILE)),
            jnp.broadcast_to(table[pl.ds(second, 1), :], (8, TILE)),
        ],
        axis=0,
    ).astype(BF16)


def row_kernel(kern_ref, count_ref, tiles_ref, mass_ref, total_ref, by_row_ref, out_ref, table, part):
    total = total_ref[...]
    table[pl.ds(0, total.shape[0]), :] = mass_ref[...] / total
    part[...] = jnp.zeros_like(part)

    def step(g, unused):
        base = g * ROW_UNROLL
        for u in range(0, ROW_UNROLL, 2):
            q = base + u
            weights = two_rows(table, tiles_ref[0, q], tiles_ref[0, q + 1])
            pair = jnp.concatenate([kern_ref[q], kern_ref[q + 1]], axis=1)
            got = dot_n(weights, pair)
            part[pl.ds(q, 1), :] = got[0:1, :TILE]
            part[pl.ds(q + 1, 1), :] = got[8:9, TILE:]
        return unused

    lax.fori_loop(0, pl.cdiv(count_ref[0, 0], ROW_UNROLL), step, 0)
    out = sum_slots(by_row_ref[...], part[...])
    out_ref[...] = poison(in_range(total, COL_LOW, COL_HIGH), out).astype(BF16)


def col_body(ok, kern_ref, count_ref, slots_ref, owners_ref, mass_ref, total, by_group_ref, out_ref, table, part):
    rows = total.shape[0]
    table[pl.ds(rows, 8), :] = jnp.zeros((8, TILE), F32)
    table[pl.ds(0, rows), :] = mass_ref[...] / total
    part[...] = jnp.zeros_like(part)
    ones = jnp.ones((16, TILE), BF16)

    def weighed(spot):
        weight = jnp.broadcast_to(table[pl.ds(owners_ref[0, spot], 1), :], (16, TILE)).astype(BF16)
        return kern_ref[slots_ref[0, spot]] * jnp.concatenate([weight] * (TILE // 16), axis=0)

    def group_sum(g):
        terms = [weighed(g * GROUP + i) for i in range(GROUP)]
        while len(terms) > 1:
            terms = [a + b for a, b in zip(terms[::2], terms[1::2], strict=True)]
        return terms[0]

    def step(i, unused):
        base = i * GROUP_UNROLL
        for u in range(0, GROUP_UNROLL, 2):
            g = base + u
            got = dot_t(ones, jnp.concatenate([group_sum(g), group_sum(g + 1)], axis=0))
            part[pl.ds(g, 1), :] = got[0:1, :TILE]
            part[pl.ds(g + 1, 1), :] = got[0:1, TILE:]
        return unused

    lax.fori_loop(0, pl.cdiv(count_ref[0, 0], GROUP_UNROLL), step, 0)
    out_ref[...] = poison(ok, sum_slots(by_group_ref[...], part[...]))


def first_col_kernel(
    kern_ref, count_ref, slots_ref, owners_ref, mass_ref, total_ref, by_group_ref, out_ref, table, part
):
    total = total_ref[...]
    ok = in_range(total, ROW_LOW, ROW_HIGH)
    col_body(ok, kern_ref, count_ref, slots_ref, owners_ref, mass_ref, total, by_group_ref, out_ref, table, part)


def next_col_kernel(
    kern_ref, count_ref, slots_ref, owners_ref, mass_ref, total_ref, earlier_ref, by_group_ref, out_ref, table, part
):
    total = total_ref[...]
    ratio = total / earlier_ref[...]
    ok = in_range(total, ROW_LOW, ROW_HIGH) & in_range(ratio, 1.0 / RATIO, RATIO)
    col_body(ok, kern_ref, count_ref, slots_ref, owners_ref, mass_ref, total, by_group_ref, out_ref, table, part)


def ring_sum(value, axis, size, perm):
    def moved(d):
        return lax.ppermute(value, axis, [(i, perm(i, d)) for i in range(size)]).astype(F32)

    opposite, right, left = moved(2), moved(1), moved(3)
    return (value.astype(F32) + opposite) + (right + left)


def sum_over_tgt(value):
    value = ring_sum(value, "tgt", 16, lambda i, d: (i // 4) * 4 + (i % 4 + d) % 4)
    value = lax.reduce_precision(value, exponent_bits=8, mantissa_bits=7).astype(BF16)
    return ring_sum(value, "tgt", 16, lambda i, d: (i + 4 * d) % 16)


def sum_over_src(value):
    value = value + lax.ppermute(value, "src", [(i, i ^ 1) for i in range(8)])
    return ring_sum(value, "src", 8, lambda i, d: (i + 2 * d) % 8)


def on_device(source_cells, target_cells, log_source, log_target, support):
    row_count = source_cells.shape[0] // TILE
    tile_count = target_cells.shape[0] // TILE
    cap = 2 * support.size // lax.axis_size("tgt")
    log_rows = log_source.reshape(row_count, TILE)
    log_cols = log_target.reshape(tile_count, TILE)
    array = jax.ShapeDtypeStruct
    groups = -(-(cap // GROUP + tile_count) // GROUP_UNROLL) * GROUP_UNROLL
    kern, total, norm, shift, mass_rows, mass_cols, tiles, count, by_row = pl.pallas_call(
        build_kernel,
        out_shape=(
            pltpu.VMEM((cap, TILE, TILE), BF16),
            array((row_count, TILE), BF16),
            array((row_count, TILE), F32),
            array((row_count, TILE), F32),
            array((row_count, TILE), F32),
            array((tile_count, TILE), F32),
            array((1, cap), jnp.int32),
            array((1, TILE), jnp.int32),
            array((row_count, cap), BF16),
        ),
        in_specs=[ANY] * 5,
        out_specs=(VMEM,) * 9,
        scratch_shapes=[
            pltpu.VMEM((tile_count, TILE, TILE), BF16),
            pltpu.VMEM((row_count, TILE), F32),
            pltpu.VMEM((cap, TILE), F32),
            pltpu.VMEM((1, cap), jnp.int32),
            pltpu.VMEM(support.shape[::-1], jnp.int32),
            pltpu.VMEM(source_cells.shape[::-1], BF16),
            pltpu.VMEM(target_cells.shape[::-1], BF16),
            pltpu.SMEM((1, cap), jnp.int32),
            pltpu.SMEM((1, cap), jnp.int32),
            pltpu.SMEM((1, TILE), jnp.int32),
            pltpu.SemaphoreType.DMA((8,)),
        ],
        compiler_params=params(20),
        name="build",
    )(support.T, source_cells.T, target_cells.T, log_rows, log_cols)
    kern = pltpu.with_memory_space_constraint(kern, pltpu.VMEM)
    slots, owners, by_group, group_count = pl.pallas_call(
        group_kernel,
        out_shape=(
            array((1, groups * GROUP), jnp.int32),
            array((1, groups * GROUP), jnp.int32),
            array((tile_count, groups), BF16),
            array((1, TILE), jnp.int32),
        ),
        in_specs=[VMEM] * 3,
        out_specs=(VMEM,) * 4,
        compiler_params=params(4),
        cost_estimate=pl.CostEstimate(flops=2 * 10**9, bytes_accessed=10**6, transcendentals=0),
        name="groups",
    )(tiles, count, by_row)

    def call(body, name, lists, vmem, out, parts):
        return pl.pallas_call(
            body,
            out_shape=out,
            in_specs=[VMEM] + [SMEM] * len(lists) + [VMEM] * len(vmem),
            out_specs=VMEM,
            scratch_shapes=[pltpu.VMEM((vmem[0].shape[0] + 8, TILE), F32), pltpu.VMEM((parts, TILE), F32)],
            compiler_params=params(20),
            name=name,
        )(kern, *lists, *vmem)

    def cols_of(body, name, totals):
        lists = (group_count, slots, owners)
        vmem = (mass_rows, *totals, by_group)
        return sum_over_src(call(body, name, lists, vmem, array((tile_count, TILE), F32), groups))

    first = sum_over_tgt(total)
    cols = cols_of(first_col_kernel, "first_col", (first,))
    rows_out = array((row_count, TILE), BF16)
    second = sum_over_tgt(call(row_kernel, "row", (count, tiles), (mass_cols, cols, by_row), rows_out, cap))
    cols = cols_of(next_col_kernel, "next_col", (second, first))
    source_pot = norm + EPS * log_rows - EPS * (jnp.log(second) + LN2 * shift)
    target_pot = EPS * log_cols - EPS * jnp.log(cols)
    return lax.cond(
        jnp.max(cols) < POISONED,
        lambda *unused: (source_pot.reshape(-1), target_pot.reshape(-1)),
        general_path,
        source_cells,
        target_cells,
        log_source,
        log_target,
        support,
    )


def solution(mesh):
    return jax.shard_map(
        on_device,
        mesh=mesh,
        in_specs=(P("src", None), P("tgt", None), P("src"), P("tgt"), P("src", None)),
        out_specs=(P("src"), P("tgt")),
        check_vma=False,
    )
```

```python
import functools

import jax
import jax.numpy as jnp
from jax import lax
from jax.experimental import pallas as pl
from jax.experimental.pallas import tpu as pltpu
from jax.sharding import PartitionSpec as P

TILE = 128
ITERS = 2


EPS = 0.1
NEG = -1e30
HIGH = lax.Precision.HIGHEST

SCALE = 14.426950408889634
LN2 = 0.6931471805599453
SHIFT = 9.0
ROW_LOW = 2.0**-24
ROW_HIGH = 2.0**80
COL_LOW = 2.0**-40
COL_HIGH = 2.0**80
RATIO = 2.0**20
POISON = 3.0e38
POISONED = 1.0e37


def squares_of(tiles):
    values = tiles.astype(jnp.float32)
    return jnp.sum(values * values, axis=2)


def cost_tile(src_block, src_square, tgt_block, tgt_square):
    cross_term = jnp.einsum(
        "bie,bje->bij", src_block, tgt_block, preferred_element_type=jnp.float32
    )
    return src_square[:, :, None] + tgt_square[:, None, :] - 2.0 * cross_term


def one_hot(ids, count):
    return (ids[:, None] == jnp.arange(count, dtype=jnp.int32)[None, :]).astype(jnp.float32)


def pick_rows(selector, table):
    return jnp.dot(selector, table, precision=HIGH, preferred_element_type=jnp.float32)


def fold_block(maxima, totals, selector, block_max, exp_of):
    candidate = jnp.max(jnp.where(selector[:, :, None] > 0.5, block_max[:, None, :], NEG), axis=0)
    new_max = jnp.maximum(maxima, candidate)
    exp_terms = exp_of(pick_rows(selector, new_max))
    added = jnp.dot(selector.T, exp_terms, precision=HIGH, preferred_element_type=jnp.float32)
    return (new_max, totals * jnp.exp(maxima - new_max) + added)


def row_stats(
    slot_rows,
    slot_tiles,
    active,
    pre_src,
    pre_srcn,
    pre_tgt,
    pre_tgtn,
    target_pot,
    row_count,
    num_blocks,
):
    shape_rows = (row_count, pre_srcn.shape[1])
    start_carry = (jnp.full(shape_rows, NEG, jnp.float32), jnp.zeros(shape_rows, jnp.float32))
    tile_count = target_pot.shape[0]

    def row_one_step(carried, block_item):
        maxima, totals = carried
        row_ids, tile_ids, alive, src_block, src_square, tgt_block, tgt_square = block_item
        costs = cost_tile(src_block, src_square, tgt_block, tgt_square)
        slot_pot = pick_rows(one_hot(tile_ids, tile_count), target_pot)
        scores = (slot_pot[:, None, :] - costs) / EPS
        block_max = jnp.where(alive[:, None], jnp.max(scores, axis=2), NEG)
        selector = one_hot(row_ids, row_count) * alive[:, None].astype(jnp.float32)

        def exp_of(slot_max):
            terms = jnp.sum(jnp.exp(scores - slot_max[:, :, None]), axis=2)
            return jnp.where(alive[:, None], terms, 0.0)

        return (fold_block(maxima, totals, selector, block_max, exp_of), None)

    def row_blocks(array):
        return array.reshape((num_blocks, -1) + array.shape[1:])

    block_items = tuple(
        (
            row_blocks(item)
            for item in (slot_rows, slot_tiles, active, pre_src, pre_srcn, pre_tgt, pre_tgtn)
        )
    )
    return lax.scan(row_one_step, start_carry, block_items)[0]


def col_stats(
    slot_rows,
    slot_tiles,
    active,
    pre_src,
    pre_srcn,
    pre_tgt,
    pre_tgtn,
    source_pot,
    tile_count,
    num_blocks,
):
    shape_cols = (tile_count, pre_tgtn.shape[1])
    start_carry = (jnp.full(shape_cols, NEG, jnp.float32), jnp.zeros(shape_cols, jnp.float32))
    row_count = source_pot.shape[0]

    def col_one_step(carried, block_item):
        maxima, totals = carried
        row_ids, tile_ids, alive, src_block, src_square, tgt_block, tgt_square = block_item
        costs = cost_tile(src_block, src_square, tgt_block, tgt_square)
        slot_pot = pick_rows(one_hot(row_ids, row_count), source_pot)
        scores = (slot_pot[:, :, None] - costs) / EPS
        block_max = jnp.where(alive[:, None], jnp.max(scores, axis=1), NEG)
        selector = one_hot(tile_ids, tile_count) * alive[:, None].astype(jnp.float32)

        def exp_of(slot_max):
            terms = jnp.sum(jnp.exp(scores - slot_max[:, None, :]), axis=1)
            return jnp.where(alive[:, None], terms, 0.0)

        return (fold_block(maxima, totals, selector, block_max, exp_of), None)

    def col_blocks(array):
        return array.reshape((num_blocks, -1) + array.shape[1:])

    block_items = tuple(
        (
            col_blocks(item)
            for item in (slot_rows, slot_tiles, active, pre_src, pre_srcn, pre_tgt, pre_tgtn)
        )
    )
    return lax.scan(col_one_step, start_carry, block_items)[0]


def across_targets(maxima, totals):
    highest = lax.pmax(maxima, "tgt")
    return (highest, lax.psum(totals * jnp.exp(maxima - highest), "tgt"))


def across_sources(maxima, totals):
    highest = lax.pmax(maxima, "src")
    return (highest, lax.psum(totals * jnp.exp(maxima - highest), "src"))


def general_path(source_cells, target_cells, log_source, log_target, support):
    row_count = source_cells.shape[0] // TILE
    src_tiles = source_cells.reshape(row_count, TILE, source_cells.shape[1])
    src_norm = squares_of(src_tiles)
    flat_ids = support.reshape(-1)
    num_slots = flat_ids.shape[0]
    tgt_index = lax.axis_index("tgt")
    own_tiles = target_cells.shape[0] // TILE
    per_device = num_slots // lax.axis_size("tgt")
    tgt_tiles = target_cells.reshape(own_tiles, TILE, target_cells.shape[1])
    log_cols = log_target.reshape(own_tiles, TILE)
    capacity = 2 * per_device
    owned = flat_ids // own_tiles == tgt_index
    slot_rank = jnp.cumsum(owned.astype(jnp.int32)) - 1
    target_place = jnp.where(owned, slot_rank, capacity)
    slot_index = (
        jnp.zeros((capacity,), jnp.int32)
        .at[target_place]
        .set(jnp.arange(num_slots, dtype=jnp.int32), mode="drop")
    )
    active = jnp.arange(capacity, dtype=jnp.int32) < jnp.sum(owned.astype(jnp.int32))
    slot_tiles = jnp.clip(flat_ids[slot_index] - tgt_index * own_tiles, 0, own_tiles - 1)
    tgt_norm = squares_of(tgt_tiles)
    tile_count = tgt_tiles.shape[0]
    slot_rows = slot_index // support.shape[1]
    pre_src = src_tiles[slot_rows]
    pre_srcn = src_norm[slot_rows]
    pre_tgt = tgt_tiles[slot_tiles]
    pre_tgtn = tgt_norm[slot_tiles]
    num_blocks = capacity // min(64, capacity)
    log_rows = log_source.reshape(row_count, TILE)
    target_pot = jnp.zeros(log_cols.shape, jnp.float32)
    source_pot = jnp.zeros(log_rows.shape, jnp.float32)
    for iteration in range(ITERS):
        maxima, totals = row_stats(
            slot_rows,
            slot_tiles,
            active,
            pre_src,
            pre_srcn,
            pre_tgt,
            pre_tgtn,
            target_pot,
            row_count,
            num_blocks,
        )
        maxima, totals = across_targets(maxima, totals)
        source_pot = EPS * log_rows - EPS * (maxima + jnp.log(totals))
        maxima, totals = col_stats(
            slot_rows,
            slot_tiles,
            active,
            pre_src,
            pre_srcn,
            pre_tgt,
            pre_tgtn,
            source_pot,
            tile_count,
            num_blocks,
        )
        maxima, totals = across_sources(maxima, totals)
        target_pot = EPS * log_cols - EPS * (maxima + jnp.log(totals))
    return (source_pot.reshape(-1), target_pot.reshape(-1))


CAP_STEP = 128
BUILD_UNROLL = 512
ROW_UNROLL = 512
GROUP = 8
GROUP_UNROLL = 64
SMEM = pl.BlockSpec(memory_space=pltpu.SMEM)
VMEM = pl.BlockSpec(memory_space=pltpu.VMEM)
ANY = pl.BlockSpec(memory_space=pl.ANY)
BF16 = jnp.bfloat16
F32 = jnp.float32


def params(mib):
    return pltpu.CompilerParams(vmem_limit_bytes=mib * 2**20)


def dot_t(a, b):
    return lax.dot_general(a, b, (((1,), (1,)), ((), ())), preferred_element_type=F32)


def dot_n(a, b):
    return jnp.dot(a, b, preferred_element_type=F32)


def ones_where(mask):
    return jnp.where(mask, 1.0, 0.0).astype(BF16)


def iota(shape, axis):
    return lax.broadcasted_iota(jnp.int32, shape, axis)


def strictly_before(size):
    return ones_where(iota((size, size), 1) < iota((size, size), 0))


def list_support(sup_ref, tiles_ref, count_ref, rows_ref, by_row_ref, own_tiles):
    width, rows = sup_ref.shape
    cap = rows_ref.shape[1]
    local = sup_ref[...] - lax.axis_index("tgt") * own_tiles
    owned = (local >= 0) & (local < own_tiles)
    mask = ones_where(owned)
    lower = ones_where(iota((width, width), 1) <= iota((width, width), 0))
    rank = dot_n(lower, mask)
    count = rank[width - 1 : width, :]
    upto = ones_where(iota((rows, rows), 1) <= iota((rows, rows), 0))
    first = jnp.sum(dot_t(strictly_before(rows), mask), axis=1, keepdims=True).astype(jnp.int32)
    last = jnp.sum(dot_t(upto, mask), axis=1, keepdims=True).astype(jnp.int32)
    place = iota((rows, cap), 1)
    by_row = ones_where((first <= place) & (place < last))
    by_row_ref[...] = by_row
    after = ones_where(iota((rows, rows), 0) < iota((rows, rows), 1))
    count8 = jnp.broadcast_to(count, (8, rows)).astype(BF16)
    first8 = dot_n(count8, after)
    high = jnp.floor(first8 * (1.0 / 32.0))
    low = first8 - 32.0 * high
    row_id = iota((8, rows), 1).astype(F32)
    tile = jnp.where(owned, local, 0).astype(F32)
    table = jnp.concatenate([tile, jnp.where(owned, rank, 0.0), row_id, high, low], axis=0)
    got = dot_n(table.astype(BF16), by_row)
    begin = 32.0 * got[2 * width + 8 : 2 * width + 9] + got[2 * width + 16 : 2 * width + 17]
    want = iota((1, cap), 1).astype(F32) - begin + 1.0
    tiles = jnp.sum(jnp.where(got[width : 2 * width] == want, got[:width], 0.0), axis=0, keepdims=True)
    tiles_ref[...] = tiles.astype(jnp.int32)
    rows_ref[...] = got[2 * width : 2 * width + 1].astype(jnp.int32)
    total = jnp.sum(count, axis=1, keepdims=True)
    count_ref[...] = jnp.broadcast_to(total, count_ref.shape).astype(jnp.int32)


def group_kernel(tiles_ref, count_ref, by_row_ref, slots_ref, owners_ref, by_group_ref, group_count_ref):
    rows, cap = by_row_ref.shape
    own_tiles, groups = by_group_ref.shape
    by_row = by_row_ref[...]
    place = iota((1, cap), 1)
    held = (iota((own_tiles, cap), 0) == tiles_ref[...]) & (place < count_ref[:, :1])
    place_f = place.astype(F32)
    by_tile = ones_where(held)
    member = dot_t(by_row, by_tile)
    rank = jnp.where(member > 0.5, dot_n(strictly_before(rows), member.astype(BF16)), 384.0).astype(BF16)
    place_high = jnp.floor(place_f * (1.0 / 32.0))
    slot_high = dot_t(by_row * place_high.astype(BF16), by_tile).astype(BF16)
    slot_low = dot_t(by_row * (place_f - 32.0 * place_high).astype(BF16), by_tile).astype(BF16)
    held_count = jnp.sum(jnp.where(held, 1.0, 0.0), axis=1, keepdims=True)
    group_count = jnp.floor((held_count + (GROUP - 1.0)) * (1.0 / GROUP))
    group_wide = jnp.broadcast_to(group_count, (own_tiles, TILE)).astype(BF16)
    begin = dot_n(strictly_before(own_tiles), group_wide)[:, :1]
    group = iota((own_tiles, groups), 1).astype(F32)
    by_group_ref[...] = ones_where((begin <= group) & (group < begin + group_count))
    spots = groups * GROUP
    spot = iota((own_tiles, spots), 1).astype(F32) - GROUP * begin
    inside = (spot >= 0.0) & (spot < held_count)
    by_spot = ones_where(inside)
    wanted = jnp.sum(jnp.where(inside, spot, 0.0), axis=0, keepdims=True)
    filled = jnp.sum(jnp.where(inside, 1.0, 0.0), axis=0, keepdims=True)
    match = (dot_n(rank, by_spot) == wanted) & (filled > 0.5)
    slot = 32.0 * dot_n(slot_high, by_spot) + dot_n(slot_low, by_spot)
    slots_ref[...] = jnp.sum(jnp.where(match, slot, 0.0), axis=0, keepdims=True).astype(jnp.int32)
    row_of = iota((rows, spots), 0).astype(F32)
    owner = jnp.sum(jnp.where(match, row_of, 0.0), axis=0, keepdims=True)
    owners_ref[...] = jnp.where(filled > 0.5, owner, float(rows)).astype(jnp.int32)
    all_groups = jnp.sum(group_count, axis=0, keepdims=True)
    group_count_ref[...] = jnp.broadcast_to(all_groups, group_count_ref.shape).astype(jnp.int32)


def sum_slots(members, parts):
    high = parts.astype(BF16)
    low = (parts - high.astype(F32)).astype(BF16)
    return dot_n(members, high) + dot_n(members, low)


def build_kernel(
    sup_hbm, src_hbm, tgt_hbm, log_rows_hbm, log_cols_hbm,
    kern_ref, sum_ref, norm_ref, shift_ref, mass_rows_ref, mass_cols_ref, tiles_out, count_out, by_row_ref,
    left, minus, part, rows_out, sup_ref, src_ref, tgt_ref, rows_ref, tiles_ref, count_ref, sems,
):
    moves = [
        pltpu.make_async_copy(*pair, sems.at[i])
        for i, pair in enumerate(
            [
                (sup_hbm, sup_ref),
                (tgt_hbm, tgt_ref),
                (src_hbm, src_ref),
                (log_rows_hbm, mass_rows_ref),
                (log_cols_hbm, mass_cols_ref),
                (rows_out, rows_ref),
                (tiles_out, tiles_ref),
                (count_out, count_ref),
            ]
        )
    ]
    for move in moves[:5]:
        move.start()
    moves[0].wait()
    dim, tgt_count = tgt_ref.shape
    list_support(sup_ref, tiles_out, count_out, rows_out, by_row_ref, tgt_count // TILE)
    for move in moves[5:]:
        move.start()
    moves[1].wait()

    def one_tgt(k, unused):
        block = tgt_ref[:, pl.ds(pl.multiple_of(k * TILE, TILE), TILE)].astype(F32)
        half = -0.5 * jnp.sum(block * block, axis=0, keepdims=True)
        first = half.astype(BF16).astype(F32)
        second = (half - first).astype(BF16).astype(F32)
        third = half - first - second
        line = iota((8, TILE), 0)
        extra = jnp.where(line == 0, first, jnp.where(line == 1, second, jnp.where(line == 2, third, 1.0)))
        extra = jnp.where(line < 4, extra, 0.0)
        none = jnp.zeros((TILE - dim - 8, TILE), F32)
        left[k] = jnp.concatenate([block, extra, none], axis=0).T.astype(BF16)
        return unused

    lax.fori_loop(0, tgt_count // TILE, one_tgt, 0, unroll=8)
    moves[2].wait()

    def eight_src(g, unused):
        norms = []
        for u in range(8):
            at = pl.multiple_of((g * 8 + u) * TILE, TILE)
            block = src_ref[:, pl.ds(at, TILE)].astype(F32)
            norms.append(jnp.sum(block * block, axis=0, keepdims=True))
        norm = jnp.concatenate(norms, axis=0)
        at = pl.multiple_of(g * 8, 8)
        norm_ref[pl.ds(at, 8), :] = norm
        part_shift = (jnp.sqrt(norm) * (SHIFT / (2.0 * SCALE))).astype(BF16).astype(F32)
        minus[pl.ds(at, 8), :] = -part_shift
        shift_ref[pl.ds(at, 8), :] = part_shift * (2.0 * SCALE)
        return unused

    lax.fori_loop(0, norm_ref.shape[0] // 8, eight_src, 0, unroll=2)
    part[...] = jnp.zeros_like(part)
    for move in moves[3:]:
        move.wait()
    mass_rows_ref[...] = jnp.exp(mass_rows_ref[...])
    mass_cols_ref[...] = jnp.exp(mass_cols_ref[...])
    line = iota((16, TILE), 0)
    pad = jnp.zeros((TILE - dim - 16, TILE), BF16)
    none = jnp.zeros((TILE, TILE), BF16)

    def right_of(q):
        r = rows_ref[0, q]
        block = src_ref[:, pl.ds(pl.multiple_of(r * TILE, TILE), TILE)]
        extra = jnp.where(line < 3, 1.0, jnp.where(line == 3, minus[pl.ds(r, 1), :], 0.0)).astype(BF16)
        return jnp.concatenate([block, extra, pad], axis=0)

    def step(g, unused):
        base = g * BUILD_UNROLL
        for u in range(0, BUILD_UNROLL, 2):
            q = base + u
            lefts = jnp.concatenate([left[tiles_ref[0, q]], left[tiles_ref[0, q + 1]]], axis=1)
            rights = jnp.concatenate(
                [
                    jnp.concatenate([right_of(q), none], axis=0),
                    jnp.concatenate([none, right_of(q + 1)], axis=0),
                ],
                axis=1,
            )
            entry = jnp.exp2(dot_n(lefts, rights) * (2.0 * SCALE))
            kern_ref[q] = entry[:, :TILE].astype(BF16)
            kern_ref[q + 1] = entry[:, TILE:].astype(BF16)
            sums = jnp.sum(entry, axis=0, keepdims=True)
            part[pl.ds(q, 1), :] = sums[:, :TILE]
            part[pl.ds(q + 1, 1), :] = sums[:, TILE:]
        return unused

    lax.fori_loop(0, pl.cdiv(count_ref[0, 0], BUILD_UNROLL), step, 0)
    sum_ref[...] = sum_slots(by_row_ref[...], part[...]).astype(BF16)


def in_range(value, low, high):
    return (value >= low) & (value <= high)


def poison(ok, value):
    bad = jnp.max(jnp.where(ok, 0.0, 1.0))
    return jnp.where(bad > 0.0, POISON, value)


def two_rows(table, first, second):
    return jnp.concatenate(
        [
            jnp.broadcast_to(table[pl.ds(first, 1), :], (8, TILE)),
            jnp.broadcast_to(table[pl.ds(second, 1), :], (8, TILE)),
        ],
        axis=0,
    ).astype(BF16)


def row_kernel(kern_ref, count_ref, tiles_ref, mass_ref, total_ref, by_row_ref, out_ref, table, part):
    total = total_ref[...]
    table[pl.ds(0, total.shape[0]), :] = mass_ref[...] / total
    part[...] = jnp.zeros_like(part)

    def step(g, unused):
        base = g * ROW_UNROLL
        for u in range(0, ROW_UNROLL, 2):
            q = base + u
            weights = two_rows(table, tiles_ref[0, q], tiles_ref[0, q + 1])
            pair = jnp.concatenate([kern_ref[q], kern_ref[q + 1]], axis=1)
            got = dot_n(weights, pair)
            part[pl.ds(q, 1), :] = got[0:1, :TILE]
            part[pl.ds(q + 1, 1), :] = got[8:9, TILE:]
        return unused

    lax.fori_loop(0, pl.cdiv(count_ref[0, 0], ROW_UNROLL), step, 0)
    out = sum_slots(by_row_ref[...], part[...])
    out_ref[...] = poison(in_range(total, COL_LOW, COL_HIGH), out).astype(BF16)


def col_body(ok, kern_ref, count_ref, slots_ref, owners_ref, mass_ref, total, by_group_ref, out_ref, table, part):
    rows = total.shape[0]
    table[pl.ds(rows, 8), :] = jnp.zeros((8, TILE), F32)
    table[pl.ds(0, rows), :] = mass_ref[...] / total
    part[...] = jnp.zeros_like(part)
    ones = jnp.ones((16, TILE), BF16)

    def weighed(spot):
        weight = jnp.broadcast_to(table[pl.ds(owners_ref[0, spot], 1), :], (16, TILE)).astype(BF16)
        return kern_ref[slots_ref[0, spot]] * jnp.concatenate([weight] * (TILE // 16), axis=0)

    def group_sum(g):
        terms = [weighed(g * GROUP + i) for i in range(GROUP)]
        while len(terms) > 1:
            terms = [a + b for a, b in zip(terms[::2], terms[1::2], strict=True)]
        return terms[0]

    def step(i, unused):
        base = i * GROUP_UNROLL
        for u in range(0, GROUP_UNROLL, 2):
            g = base + u
            got = dot_t(ones, jnp.concatenate([group_sum(g), group_sum(g + 1)], axis=0))
            part[pl.ds(g, 1), :] = got[0:1, :TILE]
            part[pl.ds(g + 1, 1), :] = got[0:1, TILE:]
        return unused

    lax.fori_loop(0, pl.cdiv(count_ref[0, 0], GROUP_UNROLL), step, 0)
    out_ref[...] = poison(ok, sum_slots(by_group_ref[...], part[...]))


def first_col_kernel(
    kern_ref, count_ref, slots_ref, owners_ref, mass_ref, total_ref, by_group_ref, out_ref, table, part
):
    total = total_ref[...]
    ok = in_range(total, ROW_LOW, ROW_HIGH)
    col_body(ok, kern_ref, count_ref, slots_ref, owners_ref, mass_ref, total, by_group_ref, out_ref, table, part)


def next_col_kernel(
    kern_ref, count_ref, slots_ref, owners_ref, mass_ref, total_ref, earlier_ref, by_group_ref, out_ref, table, part
):
    total = total_ref[...]
    ratio = total / earlier_ref[...]
    ok = in_range(total, ROW_LOW, ROW_HIGH) & in_range(ratio, 1.0 / RATIO, RATIO)
    col_body(ok, kern_ref, count_ref, slots_ref, owners_ref, mass_ref, total, by_group_ref, out_ref, table, part)


def ring_sum(value, axis, size, perm):
    def moved(d):
        return lax.ppermute(value, axis, [(i, perm(i, d)) for i in range(size)]).astype(F32)

    opposite, right, left = moved(2), moved(1), moved(3)
    return (value.astype(F32) + opposite) + (right + left)


def sum_over_tgt(value):
    value = ring_sum(value, "tgt", 16, lambda i, d: (i // 4) * 4 + (i % 4 + d) % 4)
    value = lax.reduce_precision(value, exponent_bits=8, mantissa_bits=7).astype(BF16)
    return ring_sum(value, "tgt", 16, lambda i, d: (i + 4 * d) % 16)


def sum_over_src(value):
    value = value + lax.ppermute(value, "src", [(i, i ^ 1) for i in range(8)])
    return ring_sum(value, "src", 8, lambda i, d: (i + 2 * d) % 8)


def on_device(source_cells, target_cells, log_source, log_target, support):
    row_count = source_cells.shape[0] // TILE
    tile_count = target_cells.shape[0] // TILE
    cap = 2 * support.size // lax.axis_size("tgt")
    log_rows = log_source.reshape(row_count, TILE)
    log_cols = log_target.reshape(tile_count, TILE)
    array = jax.ShapeDtypeStruct
    groups = -(-(cap // GROUP + tile_count) // GROUP_UNROLL) * GROUP_UNROLL
    kern, total, norm, shift, mass_rows, mass_cols, tiles, count, by_row = pl.pallas_call(
        build_kernel,
        out_shape=(
            pltpu.VMEM((cap, TILE, TILE), BF16),
            array((row_count, TILE), BF16),
            array((row_count, TILE), F32),
            array((row_count, TILE), F32),
            array((row_count, TILE), F32),
            array((tile_count, TILE), F32),
            array((1, cap), jnp.int32),
            array((1, TILE), jnp.int32),
            array((row_count, cap), BF16),
        ),
        in_specs=[ANY] * 5,
        out_specs=(VMEM,) * 9,
        scratch_shapes=[
            pltpu.VMEM((tile_count, TILE, TILE), BF16),
            pltpu.VMEM((row_count, TILE), F32),
            pltpu.VMEM((cap, TILE), F32),
            pltpu.VMEM((1, cap), jnp.int32),
            pltpu.VMEM(support.shape[::-1], jnp.int32),
            pltpu.VMEM(source_cells.shape[::-1], BF16),
            pltpu.VMEM(target_cells.shape[::-1], BF16),
            pltpu.SMEM((1, cap), jnp.int32),
            pltpu.SMEM((1, cap), jnp.int32),
            pltpu.SMEM((1, TILE), jnp.int32),
            pltpu.SemaphoreType.DMA((8,)),
        ],
        compiler_params=params(20),
        name="build",
    )(support.T, source_cells.T, target_cells.T, log_rows, log_cols)
    kern = pltpu.with_memory_space_constraint(kern, pltpu.VMEM)
    slots, owners, by_group, group_count = pl.pallas_call(
        group_kernel,
        out_shape=(
            array((1, groups * GROUP), jnp.int32),
            array((1, groups * GROUP), jnp.int32),
            array((tile_count, groups), BF16),
            array((1, TILE), jnp.int32),
        ),
        in_specs=[VMEM] * 3,
        out_specs=(VMEM,) * 4,
        compiler_params=params(4),
        cost_estimate=pl.CostEstimate(flops=2 * 10**9, bytes_accessed=10**6, transcendentals=0),
        name="groups",
    )(tiles, count, by_row)

    def call(body, name, lists, vmem, out, parts):
        return pl.pallas_call(
            body,
            out_shape=out,
            in_specs=[VMEM] + [SMEM] * len(lists) + [VMEM] * len(vmem),
            out_specs=VMEM,
            scratch_shapes=[pltpu.VMEM((vmem[0].shape[0] + 8, TILE), F32), pltpu.VMEM((parts, TILE), F32)],
            compiler_params=params(20),
            name=name,
        )(kern, *lists, *vmem)

    def cols_of(body, name, totals):
        lists = (group_count, slots, owners)
        vmem = (mass_rows, *totals, by_group)
        return sum_over_src(call(body, name, lists, vmem, array((tile_count, TILE), F32), groups))

    first = sum_over_tgt(total)
    cols = cols_of(first_col_kernel, "first_col", (first,))
    rows_out = array((row_count, TILE), BF16)
    second = sum_over_tgt(call(row_kernel, "row", (count, tiles), (mass_cols, cols, by_row), rows_out, cap))
    cols = cols_of(next_col_kernel, "next_col", (second, first))
    source_pot = norm + EPS * log_rows - EPS * (jnp.log(second) + LN2 * shift)
    target_pot = EPS * log_cols - EPS * jnp.log(cols)
    return lax.cond(
        jnp.max(cols) < POISONED,
        lambda *unused: (source_pot.reshape(-1), target_pot.reshape(-1)),
        general_path,
        source_cells,
        target_cells,
        log_source,
        log_target,
        support,
    )


def solution(mesh):
    return jax.shard_map(
        on_device,
        mesh=mesh,
        in_specs=(P("src", None), P("tgt", None), P("src"), P("tgt"), P("src", None)),
        out_specs=(P("src"), P("tgt")),
        check_vma=False,
    )
```
